128 devices in a mesh: grp: 2 (over z_lo), dp: 4 (over y), mp: 16 (over x, z_hi, core).
Axes of the slice: x: 4, y: 4, z: 4 (z_hi: 2, z_lo: 2; z = z_hi * 2 + z_lo), core: 2. Of those that a mesh axis runs over, the one named last changes fastest.
Arguments:
- queries: bfloat16 [4, 2048, 4096], P('dp', None, 'mp'), may hold values from -5 to 5
- keys: bfloat16 [4, 2048, 512], P('dp'), may hold values from -5 to 5
- values: bfloat16 [4, 2048, 512], P('dp'), may hold values from -6 to 6
- out_weight: bfloat16 [4096, 5120], P('mp'), may hold values from -0.09375 to 0.09375
- residual: bfloat16 [4, 2048, 5120], P('dp', 'mp'), may hold values from -24 to 24
- student_hidden: bfloat16 [4, 2048, 2560], P('dp', 'mp'), may hold values from -6 to 6
- norm_gain: float32 [2560], replicated, may hold values from 0.5 to 1.5
- projection: bfloat16 [2560, 5120], P(None, ('grp', 'dp')), may hold values from -0.125 to 0.125
- lengths: int32 [4], replicated, may hold values from 512 to 2048, as said below
Outputs:
- teacher_out: bfloat16 [4, 2048, 5120], P('dp', 'mp', 'grp')
- distill_loss: float32 [], replicated
- grad_proj: float32 [2560, 5120], P('mp', ('grp', 'dp'))
- grad_gain: float32 [2560], P('grp')
- grad_hidden: float32 [4, 2048, 2560], P('dp', 'mp', 'grp')
The draws below stay inside these ranges and needn't reach their ends.
Inputs may be any that keep to these rules, and one draw needn't show every extreme that they name: `lengths`: at least one sequence is live throughout.
All inputs are finite; a program needn't handle non-finite values.
Results may differ from the reference program's by a relative error of at most 0.018.
Values may be sent and summed in bfloat16 or wider, within the bound.
No kernel may reach another device: no remote copies, remote signals or barrier semaphores. Data moves between devices by JAX's collectives and lax.ppermute only.
A program may use at most 128 MiB of HBM per device.

```python
import jax
import jax.numpy as jnp
from jax import lax

D_T = 5120
D_S = 2560
HD = 128
HQ = 32
KVH = 4
L = 2048
SEQS = 4
N_MP = 16


def draw_keys(key, part):
    key = jax.random.fold_in(key, 7)
    sampled = jax.random.truncated_normal(key, -5.0, 5.0, (SEQS, L, KVH * HD), jnp.float32)
    return sampled.astype(jnp.bfloat16)


def draw_queries(key, part):
    key = jax.random.fold_in(key, 9)
    sampled = jax.random.truncated_normal(key, -5.0, 5.0, (SEQS, L, HQ * HD), jnp.float32)
    return sampled.astype(jnp.bfloat16)


def column_scales(low, high):
    ramp = jnp.arange(D_T, dtype=jnp.float32) / (D_T - 1)
    return jnp.exp(jnp.log(low) + ramp * (jnp.log(high) - jnp.log(low)))


def draw_residual(key, part):
    key = jax.random.fold_in(key, 11)
    sampled = jax.random.truncated_normal(key, -6.0, 6.0, (SEQS, L, D_T), jnp.float32)
    scales = column_scales(0.5, 3.0)
    return (sampled * scales[None, None, :]).astype(jnp.bfloat16)


def draw_lengths(key, part):
    key = jax.random.fold_in(key, 5)
    first_key, second_key = jax.random.split(key)
    sampled = jax.random.randint(first_key, (SEQS,), L // 4, L + 1)
    full_index = jax.random.randint(second_key, (), 0, SEQS)
    return jnp.where(jnp.arange(SEQS) == full_index, L, sampled).astype(jnp.int32)


def shard_levels(key, extent, shards, low, high):
    loudness = 1.0
    for dim, shards_of in shards:
        steps = jax.random.uniform(jax.random.fold_in(jax.random.fold_in(key, 6), dim), (shards_of,), jnp.float32, low / len(shards), high / len(shards))
        loudness = loudness * jnp.repeat(jnp.exp(steps), extent[dim] // shards_of).reshape((-1,) + (1,) * (len(extent) - 1 - dim))
    return loudness


def noise(rng, dims, width, most, shards=(), held_as=jnp.bfloat16):
    level = shard_levels(rng, dims, shards, -0.22, 0.18) if shards else 1.0
    entries = jax.random.normal(rng, dims, jnp.float32) * width * level
    return jnp.minimum(jnp.maximum(entries, -most), most).astype(held_as)


def setup_inputs(seed: int = 0) -> dict:
    key_of = jax.random.split(jax.random.key(seed), 10)
    queries = draw_queries(jax.random.fold_in(key_of[9], 71), 0)
    keys = draw_keys(jax.random.fold_in(key_of[9], 71), 0)
    values = noise(key_of[2], (SEQS, L, KVH * HD), 1.0, 6.0, ((0, 4),))
    out_weight = noise(key_of[3], (HQ * HD, D_T), (HQ * HD) ** -0.5, 0.09375, ((0, 16),))
    residual = draw_residual(jax.random.fold_in(key_of[9], 71), 0)
    student_hidden = noise(key_of[5], (SEQS, L, D_S), 1.0, 6.0, ((0, 4), (1, 16)))
    norm_gain = jnp.clip(1.0 + 0.1 * jax.random.normal(key_of[6], (D_S,), jnp.float32), 0.5, 1.5)
    projection = noise(key_of[7], (D_S, D_T), D_S ** -0.5, 0.125, ((1, 8),))
    lengths = draw_lengths(jax.random.fold_in(key_of[9], 71), 0)
    return dict(queries=queries, keys=keys, values=values, out_weight=out_weight, residual=residual, student_hidden=student_hidden, norm_gain=norm_gain, projection=projection, lengths=lengths)


def attend_heads(query_heads, key_heads, value_heads):
    seq_len = query_heads.shape[0]
    positions = jnp.arange(seq_len, dtype=jnp.int32)
    scores = jnp.einsum('qgd,kgd->gqk', query_heads.astype(jnp.float32), key_heads.astype(jnp.float32)) * HD ** (-0.5)
    allowed = positions[None, :, None] >= positions[None, None, :]
    scores = jnp.where(allowed, scores, -1e+30)
    row_max = lax.optimization_barrier(jnp.max(scores, axis=-1, keepdims=True))
    exponent = jnp.exp(scores - row_max)
    weights = (exponent / lax.optimization_barrier(jnp.sum(exponent, axis=-1, keepdims=True))).astype(jnp.bfloat16)
    context = jnp.einsum('gqk,kgd->qgd', weights.astype(jnp.float32), value_heads.astype(jnp.float32))
    return context.reshape(seq_len, -1).astype(jnp.bfloat16)

def teacher_rows(query_seq, key_seq, value_seq, out_weight, residual_seq):
    seq_len = query_seq.shape[0]
    group_heads = HQ // N_MP
    shared = HQ // KVH
    query_groups = query_seq.reshape(seq_len, N_MP, group_heads, HD).transpose(1, 0, 2, 3)
    weight_groups = out_weight.reshape(N_MP, group_heads * HD, D_T)
    key_heads = key_seq.reshape(seq_len, KVH, HD)
    value_heads = value_seq.reshape(seq_len, KVH, HD)

    def add_group(summed, inputs):
        query_group, weight_group, group_index = inputs
        kv_index = ((group_index * group_heads + jnp.arange(group_heads, dtype=jnp.int32)) // shared).astype(jnp.int32)
        context = attend_heads(query_group, jnp.take(key_heads, kv_index, axis=1), jnp.take(value_heads, kv_index, axis=1))
        partial_sum = jnp.dot(context, weight_group, preferred_element_type=jnp.float32).astype(jnp.bfloat16)
        partial_sum = lax.optimization_barrier(partial_sum)
        return (summed + partial_sum.astype(jnp.float32), None)
    summed, unused = lax.scan(add_group, jnp.zeros((seq_len, D_T), jnp.float32), (query_groups, weight_groups, jnp.arange(N_MP, dtype=jnp.int32)))
    return (residual_seq.astype(jnp.float32) + summed).astype(jnp.bfloat16)

def reference(queries, keys, values, out_weight, residual, student_hidden, norm_gain, projection, lengths):
    teacher_out = jnp.stack([teacher_rows(queries[sequence], keys[sequence], values[sequence], out_weight, residual[sequence]) for sequence in range(SEQS)])
    hidden = student_hidden.reshape(-1, D_S).astype(jnp.float32)
    inverse_rms = lax.rsqrt(lax.optimization_barrier(jnp.mean(hidden * hidden, axis=-1, keepdims=True)) + 1e-06)
    unit = hidden * inverse_rms
    normed = (unit * norm_gain).astype(jnp.bfloat16)
    predicted = jnp.dot(normed, projection, preferred_element_type=jnp.float32)
    positions = jnp.arange(L, dtype=jnp.int32)
    live_rows = (positions[None, :] < lengths[:, None]).reshape(-1, 1)
    live_count = jnp.sum(lengths).astype(jnp.float32)
    difference = jnp.where(live_rows, predicted - teacher_out.reshape(-1, D_T).astype(jnp.float32), 0.0)
    distill_loss = jnp.sum(difference * difference) / (live_count * D_T)
    grad_pred = difference.astype(jnp.bfloat16)
    grad_proj = lax.dot_general(normed, grad_pred, (((0,), (0,)), ((), ())), preferred_element_type=jnp.float32) / live_count
    grad_normed = lax.dot_general(grad_pred, projection, (((1,), (1,)), ((), ())), preferred_element_type=jnp.float32)
    grad_gain = lax.optimization_barrier(jnp.sum(grad_normed * unit, axis=0)) / live_count
    scaled = grad_normed * norm_gain
    mean_term = lax.optimization_barrier(jnp.sum(scaled * unit, axis=-1, keepdims=True)) / D_S
    grad_hidden = inverse_rms * (scaled - unit * mean_term)
    return (teacher_out, distill_loss, grad_proj, grad_gain, grad_hidden.reshape(SEQS, L, D_S))
```

```python
import functools
import math

import jax
import jax.numpy as jnp
from jax import lax
from jax.experimental import pallas as pl
from jax.experimental.pallas import tpu as pltpu
from jax.sharding import Mesh
from jax.sharding import PartitionSpec as P

D_T = 5120
D_S = 2560
HD = 128
HQ = 32
KVH = 4

BF = jnp.bfloat16
F32 = jnp.float32
NX = 4
NZ = 4
MP = ("x", "zh", "core")


def ring(n, k):
    return [(i, (i + k) % n) for i in range(n)]


WRAP = [(g * 2 + z, (1 - g) * 2 + (1 - z)) for g in range(2) for z in range(2)]
WRAP_CORE = [
    (g * 4 + z * 2 + c, (1 - g) * 4 + (1 - z) * 2 + (1 - c))
    for g in range(2)
    for z in range(2)
    for c in range(2)
]


def attend_kernel(scalars, q0_ref, q1_ref, k_ref, v_ref, out_ref, vext):
    first = scalars[1] * 128
    vext[:, :HD] = v_ref[...]
    vext[:, HD:] = jnp.ones((v_ref.shape[0], HD), BF)
    scale = HD ** (-0.5) * math.log2(math.e)
    rows = lax.broadcasted_iota(jnp.int32, (256, 512), 0) % 128
    cols = lax.broadcasted_iota(jnp.int32, (256, 512), 1)
    allowed = cols <= rows + first
    for part in range(NX):
        length = 512 * (part + 1)
        for pair, q_ref in enumerate((q0_ref, q1_ref)):
            q = jnp.concatenate([q_ref[part, :, :HD], q_ref[part, :, HD:]], axis=0)
            scores = lax.dot_general(
                q, k_ref[:length, :], (((1,), (1,)), ((), ())), preferred_element_type=F32
            )
            last = jnp.where(allowed, scores[:, length - 512 :], -1e30)
            if part:
                scores = jnp.concatenate([scores[:, : length - 512], last], axis=1)
            else:
                scores = last
            top = jnp.max(scores, axis=-1, keepdims=True)
            probs = jnp.exp2((scores - top) * scale).astype(BF)
            mixed = jnp.dot(probs, vext[:length, :], preferred_element_type=F32)
            mixed = (mixed[:, :HD] / mixed[:, HD:]).astype(BF)
            for head in range(2):
                at = (pair * 2 + head) * HD
                out_ref[part * 128 : part * 128 + 128, at : at + HD] = mixed[
                    head * 128 : head * 128 + 128
                ]


def attend(scalars, q0, q1, keys, values):
    seq_len = keys.shape[0]
    return pl.pallas_call(
        attend_kernel,
        out_shape=jax.ShapeDtypeStruct((NX * 128, 4 * HD), BF),
        grid_spec=pltpu.PrefetchScalarGridSpec(
            num_scalar_prefetch=1,
            grid=(1,),
            in_specs=[
                pl.BlockSpec((NX, 128, 256), lambda i, s: (0, 0, 0)),
                pl.BlockSpec((NX, 128, 256), lambda i, s: (0, 0, 0)),
                pl.BlockSpec((seq_len, HD), lambda i, s: (0, s[0])),
                pl.BlockSpec((seq_len, HD), lambda i, s: (0, s[0])),
            ],
            out_specs=pl.BlockSpec((NX * 128, 4 * HD), lambda i, s: (0, 0)),
            scratch_shapes=[pltpu.VMEM((seq_len, 2 * HD), BF)],
        ),
        compiler_params=pltpu.CompilerParams(vmem_limit_bytes=40 * 1024 * 1024),
        cost_estimate=pl.CostEstimate(
            flops=4 * 512 * 4 * 1280 * HD * 2, bytes_accessed=2 * 1024 * 1024, transcendentals=2621440
        ),
        name="attend",
    )(scalars, q0, q1, keys, values)


def body(
    queries, keys, values, out_weight, residual, student_hidden, norm_gain, projection, lengths
):
    g, d = lax.axis_index("grp"), lax.axis_index("dp")
    x, zh, c = lax.axis_index("x"), lax.axis_index("zh"), lax.axis_index("core")
    zc = zh * 2 + c
    m = x * 4 + zc
    half = D_T // 2
    blk = D_T // 8

    q4 = queries[0].reshape(NX, 512, 256)

    def q_for(block):
        return lax.dynamic_slice_in_dim(q4, block * 128, 128, 1)

    q_own = q_for(zc)
    q_core = lax.ppermute(q_for(zh * 2 + 1 - c), "core", ring(2, 1))
    q_z0 = lax.ppermute(q_for((1 - zh) * 2 + c), ("grp", "zh"), WRAP)
    q_z1 = lax.ppermute(q_for((1 - zh) * 2 + 1 - c), ("grp", "zh", "core"), WRAP_CORE)

    w_own = lax.dynamic_slice_in_dim(out_weight, g * half, half, 1)
    w_sent = lax.dynamic_slice_in_dim(out_weight, (1 - g) * half, half, 1)
    w_core = lax.ppermute(w_own, "core", ring(2, 1))
    w_z0 = lax.ppermute(w_sent, ("grp", "zh"), WRAP)
    w_z1 = lax.ppermute(w_z0, "core", ring(2, 1))

    hidden = student_hidden[0].astype(F32)
    inverse_rms = lax.rsqrt(jnp.mean(hidden * hidden, axis=-1, keepdims=True) + 1e-06)
    unit_rows = hidden * inverse_rms
    scaled_rows = unit_rows * norm_gain
    normed = scaled_rows.astype(BF)
    normed_all = lax.all_gather(normed, "dp", axis=0, tiled=True)
    predicted = jnp.dot(normed_all, projection, preferred_element_type=F32)

    scalars = jnp.stack([x, zc]).astype(jnp.int32)
    ctx_a = attend(scalars, q_own, q_core, keys[0], values[0])
    ctx_b = attend(scalars, q_z0, q_z1, keys[0], values[0])
    weight = jnp.concatenate([w_own, w_core, w_z0, w_z1], axis=0)
    ctx = jnp.concatenate([ctx_a, ctx_b], axis=1)

    live_count = jnp.sum(lengths).astype(F32)
    positions = m * 128 + jnp.arange(128, dtype=jnp.int32)
    squared = jnp.zeros((), F32)
    gain_part = jnp.zeros((D_S,), F32)
    summed = jnp.zeros((128, D_S), F32)
    target = jnp.zeros((128, half), BF)
    grad_pred = jnp.zeros((512, blk), BF)
    for k in (2, 1, 3, 0):
        at = ((d + k) % 4) * blk
        part = jnp.dot(
            ctx, lax.dynamic_slice_in_dim(weight, at, blk, 1), preferred_element_type=F32
        ).astype(BF).reshape(NX, 128, blk)
        rows = lax.dynamic_index_in_dim(part, x, 0, keepdims=False).astype(F32)
        for j in (2, 1, 3):
            piece = lax.dynamic_index_in_dim(part, (x + j) % NX, 0, keepdims=False)
            rows = rows + lax.ppermute(piece, "x", ring(NX, j)).astype(F32)
        res = lax.dynamic_slice_in_dim(residual[0], g * half + at, blk, 1)
        done = (res.astype(F32) + rows).astype(BF)
        target = lax.dynamic_update_slice_in_dim(target, done, at, 1)
        got = done if k == 0 else lax.ppermute(done, "dp", ring(4, k))
        seq = (d + 4 - k) % 4
        live = (positions < lax.dynamic_index_in_dim(lengths, seq, 0, keepdims=False))[:, None]
        pred = lax.dynamic_slice_in_dim(predicted, seq * 128, 128, 0)
        diff = jnp.where(live, pred - got.astype(F32), 0.0)
        squared = squared + jnp.sum(diff * diff)
        gp = diff.astype(BF)
        grad_pred = lax.dynamic_update_slice_in_dim(grad_pred, gp, seq * 128, 0)
        back = lax.dot_general(
            gp, projection, (((1,), (1,)), ((), ())), preferred_element_type=F32
        )
        normed_seq = lax.dynamic_slice_in_dim(normed_all, seq * 128, 128, 0)
        gain_part = gain_part + jnp.sum(back * normed_seq.astype(F32), axis=0)
        if k == 0:
            summed = summed + back
        else:
            summed = summed + lax.ppermute(back.astype(BF), "dp", ring(4, 4 - k)).astype(F32)

    small = jnp.concatenate([gain_part / norm_gain, jnp.full((128,), squared)])
    small = small.reshape(-1, 128)
    small = small + lax.ppermute(small, "core", ring(2, 1))
    for axis, n in (("x", 4), ("dp", 4), (("grp", "zh"), 4)):
        small = sum([lax.ppermute(small, axis, ring(n, j)) for j in range(1, n)], small)
    small = small.reshape(-1)
    distill_loss = small[D_S] / (live_count * D_T)
    grad_gain = lax.dynamic_slice_in_dim(small, g * (D_S // 2), D_S // 2, 0) / live_count

    gproj = lax.dot_general(
        normed_all, grad_pred, (((0,), (0,)), ((), ())), preferred_element_type=F32
    ).astype(BF).reshape(NX, 2, 2, D_S // 16, blk)
    take = functools.partial(lax.dynamic_index_in_dim, keepdims=False)
    gproj = (
        take(gproj, c, 2).astype(F32)
        + lax.ppermute(take(gproj, 1 - c, 2), "core", ring(2, 1)).astype(F32)
    ).astype(BF)
    acc = take(gproj, x, 0).astype(F32)
    for j in (2, 1, 3):
        acc = acc + lax.ppermute(take(gproj, (x + j) % NX, 0), "x", ring(NX, j)).astype(F32)
    acc16 = acc.astype(BF)
    grad_proj = (
        take(acc, zh, 0) + lax.ppermute(take(acc16, 1 - zh, 0), "zh", ring(2, 1)).astype(F32)
    ) / live_count

    width = D_S // 2
    inner = jnp.sum(summed * scaled_rows, axis=-1)
    inner = inner + lax.ppermute(inner, "grp", ring(2, 1))
    sent = lax.dynamic_slice_in_dim(summed, (1 - g) * width, width, 1).astype(BF)
    kept = lax.dynamic_slice_in_dim(summed, g * width, width, 1)
    grad_half = kept + lax.ppermute(sent, "grp", ring(2, 1)).astype(F32)
    gain_half = lax.dynamic_slice_in_dim(norm_gain, g * width, width, 0)
    unit_half = lax.dynamic_slice_in_dim(unit_rows, g * width, width, 1)
    mean_term = (inner / D_S)[:, None]
    grad_hidden = inverse_rms * (grad_half * gain_half - unit_half * mean_term)
    return (target[None], distill_loss, grad_proj, grad_gain, grad_hidden[None])


def solution(mesh):
    fine = Mesh(mesh.devices.reshape(2, 4, 4, 2, 2), ("grp", "dp", "x", "zh", "core"))
    in_specs = (
        P("dp", None, MP),
        P("dp", None, None),
        P("dp", None, None),
        P(MP, None),
        P("dp", MP, None),
        P("dp", MP, None),
        P(),
        P(None, ("grp", "dp")),
        P(),
    )
    out_specs = (P("dp", MP, "grp"), P(), P(MP, ("grp", "dp")), P("grp"), P("dp", MP, "grp"))
    return jax.shard_map(body, mesh=fine, in_specs=in_specs, out_specs=out_specs, check_vma=False)
```

```python
import math

import jax
import jax.numpy as jnp
from jax import lax
from jax.experimental import pallas as pl
from jax.experimental.pallas import tpu as pltpu
from jax.sharding import Mesh
from jax.sharding import PartitionSpec as P

D_T = 5120
D_S = 2560
HD = 128
HQ = 32
KVH = 4

BF = jnp.bfloat16
F32 = jnp.float32
NX = 4
NZ = 4
MP = ("x", "zh", "core")


def ring(n, k):
    return [(i, (i + k) % n) for i in range(n)]


WRAP = [(g * 2 + z, (1 - g) * 2 + (1 - z)) for g in range(2) for z in range(2)]
WRAP_CORE = [
    (g * 4 + z * 2 + c, (1 - g) * 4 + (1 - z) * 2 + (1 - c))
    for g in range(2)
    for z in range(2)
    for c in range(2)
]


MIB = 32
COST = 1
STEPS = (0, 10, 1, 11)
STAGES = ((2, 1), (3, 0))
ORDER = sum(STAGES, ())


def whole(shape):
    return pl.BlockSpec(shape, lambda i, s: (0,) * len(shape))


def call(kernel, scalars, ins, outs, name, scratch=(), mib=MIB):
    outs = pl.pallas_call(
        kernel,
        out_shape=[jax.ShapeDtypeStruct(shape, t) for shape, t in outs],
        grid_spec=pltpu.PrefetchScalarGridSpec(
            num_scalar_prefetch=1,
            grid=(1,),
            in_specs=[spec for _, spec in ins],
            out_specs=[whole(shape) for shape, _ in outs],
            scratch_shapes=list(scratch),
        ),
        compiler_params=pltpu.CompilerParams(vmem_limit_bytes=mib * 1024 * 1024),
        cost_estimate=pl.CostEstimate(flops=COST, bytes_accessed=COST, transcendentals=0),
        name=name,
    )(scalars.value, *[a for a, _ in ins])
    scalars.after(outs[0])
    return outs


class Ordered:
    def __init__(self, value):
        self.value = value

    def after(self, array):
        self.value, _ = lax.optimization_barrier((self.value, array))


X, ZC, G, D, ZH, C, FIRST, LENGTHS = range(8)


def pick_kernel(s, q1, q2, q3, *refs):
    o1, o2, o3 = refs[4:7]
    o1[...] = q1[:, 0]
    o2[...] = q2[:, 0]
    o3[...] = q3[:, 0]
    pieces = list(refs[:4])
    for ks, out in zip(STAGES, refs[7:]):
        for i in range(len(ks)):
            out[:, i * 640 : i * 640 + 640] = pieces.pop(0)[...]


def attend_kernel(scalars, q0_ref, q1_ref, k_ref, v_ref, out_ref, vext):
    first = scalars[ZC] * 128
    vext[:, :HD] = v_ref[...]
    vext[:, HD:] = jnp.ones((v_ref.shape[0], HD), BF)
    scale = HD ** (-0.5) * math.log2(math.e)
    rows = lax.broadcasted_iota(jnp.int32, (256, 512), 0) % 128
    cols = lax.broadcasted_iota(jnp.int32, (256, 512), 1)
    allowed = cols <= rows + first
    for part in range(NX):
        length = 512 * (part + 1)
        for pair, q_ref in enumerate((q0_ref, q1_ref)):
            q = q_ref[part] if len(q_ref.shape) == 3 else q_ref[part, 0]
            q = jnp.concatenate([q[:, :HD], q[:, HD:]], axis=0)
            scores = lax.dot_general(
                q, k_ref[:length, :], (((1,), (1,)), ((), ())), preferred_element_type=F32
            )
            last = jnp.where(allowed, scores[:, length - 512 :], -1e30)
            if part:
                scores = jnp.concatenate([scores[:, : length - 512], last], axis=1)
            else:
                scores = last
            top = jnp.max(scores, axis=-1, keepdims=True)
            probs = jnp.exp2((scores - top) * scale).astype(BF)
            mixed = jnp.dot(probs, vext[:length, :], preferred_element_type=F32)
            mixed = (mixed[:, :HD] / mixed[:, HD:]).astype(BF)
            for head in range(2):
                at = (pair * 2 + head) * HD
                out_ref[part * 128 : part * 128 + 128, at : at + HD] = mixed[
                    head * 128 : head * 128 + 128
                ]


def project_kernel(s, ctx_a, ctx_b, w2, w3, *refs):
    own, o1, o2, o3, total = refs[-5:]
    n = len(refs[:-5]) // 2

    def dot(a, b):
        return jnp.dot(a, b, preferred_element_type=F32)

    for part, (w0, w1) in enumerate(zip(refs[:n], refs[n : 2 * n])):
        cols = slice(part * 640, part * 640 + 640)
        total[:, cols] = (
            dot(ctx_a[:, :256], w0[...])
            + dot(ctx_a[:, 256:], w1[...])
            + dot(ctx_b[:, :256], w2[:, cols])
            + dot(ctx_b[:, 256:], w3[:, cols])
        )
    for j, out in enumerate((own, o1, o2, o3)):
        at = pl.multiple_of(((s[X] + j) % NX) * 128, 128)
        out[...] = total[pl.ds(at, 128), :].astype(out.dtype)


def finish_kernel(s, own, r1, r2, r3, *refs):
    n = own.shape[1] // 640
    rows = own[...] + r1[...].astype(F32) + r2[...].astype(F32) + r3[...].astype(F32)
    olds, target = [], None
    if len(refs) > 2 * n:
        olds, target = refs[n : -n - 1], refs[-1]
    news = refs[-n - 1 : -1] if olds else refs[-n:]
    for i in range(n):
        news[i][...] = (refs[i][...].astype(F32) + rows[:, i * 640 : i * 640 + 640]).astype(BF)
    for k, done in zip(ORDER, (*olds, *news) if olds else ()):
        at = pl.multiple_of(((s[D] + k) % 4) * 640, 128)
        target[:, pl.ds(at, 640)] = done[...]


def compare_kernel(ks, s, pred, normed, proj, *refs):
    n = len(ks)
    gots, gps, backs, (gain, loss, both) = refs[:n], refs[n : 2 * n], refs[2 * n : 3 * n], refs[3 * n :]
    square = jnp.zeros((1, 640), F32)
    starts = []
    for i, (k, got, gp) in enumerate(zip(ks, gots, gps)):
        seq = (s[D] + 4 - k) % 4
        at = pl.multiple_of(seq * 128, 128)
        starts.append(at)
        live = lax.broadcasted_iota(jnp.int32, (128, 640), 0) < s[LENGTHS + seq] - s[FIRST]
        diff = jnp.where(live, pred[pl.ds(at, 128), :] - got[...].astype(F32), 0.0)
        square = square + jnp.sum(diff * diff, axis=0, keepdims=True)
        rounded = diff.astype(BF)
        gp[...] = rounded
        both[i * 128 : i * 128 + 128] = rounded
    loss[...] = square
    for part in range(4):
        cols = slice(part * 640, part * 640 + 640)
        grad = lax.dot_general(
            both[...], proj[cols, :], (((1,), (1,)), ((), ())), preferred_element_type=F32
        )
        total = jnp.zeros((128, 640), F32)
        for i, (at, back) in enumerate(zip(starts, backs)):
            rows = grad[i * 128 : i * 128 + 128]
            back[:, cols] = rows.astype(back.dtype)
            total = total + rows * normed[pl.ds(at, 128), cols].astype(F32)
        gain[:, cols] = jnp.sum(total, axis=0, keepdims=True)


def combine_kernel(s, own, r1, r2, r3, scaled, sent, kept, inner):
    total = own[...] + r1[...].astype(F32) + r2[...].astype(F32) + r3[...].astype(F32)
    inner[...] = jnp.sum(total * scaled[...], axis=-1, keepdims=True)
    width = D_S // 2
    first = s[G] == 0
    kept[...] = jnp.where(first, total[:, :width], total[:, width:])
    sent[...] = jnp.where(first, total[:, width:], total[:, :width]).astype(BF)


def gproj_kernel(s, normed, gp2, gp1, gp3, gp0, sent, kept, gp):
    for k, part in zip((2, 1, 3, 0), (gp2, gp1, gp3, gp0)):
        at = pl.multiple_of(((s[D] + 4 - k) % 4) * 128, 128)
        gp[pl.ds(at, 128), :] = part[...]
    first = s[C] == 0
    for part in range(NX):
        total = lax.dot_general(
            normed[:, part * 640 : part * 640 + 640],
            gp[...],
            (((0,), (0,)), ((), ())),
            preferred_element_type=F32,
        )
        for z in range(2):
            low = total[z * 320 : z * 320 + 160]
            high = total[z * 320 + 160 : z * 320 + 320]
            sent[part, z] = jnp.where(first, high, low).astype(BF)
            kept[part, z] = jnp.where(first, low, high)


def gproj_add_kernel(s, kept, recv, own, o1, o2, o3):
    for j, out in enumerate((own, o1, o2, o3)):
        at = (s[X] + j) % NX
        out[...] = (kept[at] + recv[at].astype(F32)).astype(out.dtype)


def gproj_sum_kernel(s, own, r1, r2, r3, sent, kept):
    z = s[ZH]

    def total(at):
        return own[at] + r1[at].astype(F32) + r2[at].astype(F32) + r3[at].astype(F32)

    sent[...] = total(1 - z).astype(BF)
    kept[...] = total(z)


def body(
    queries, keys, values, out_weight, residual, student_hidden, norm_gain, projection, lengths
):
    g, d = lax.axis_index("grp"), lax.axis_index("dp")
    x, zh, c = lax.axis_index("x"), lax.axis_index("zh"), lax.axis_index("core")
    zc = zh * 2 + c
    m = x * 4 + zc
    half = D_T // 2
    blk = D_T // 8
    rows = D_S // 16
    barrier = lax.optimization_barrier
    scalars = Ordered(
        jnp.concatenate([jnp.stack([x, zc, g, d, zh, c, m * 128]).astype(jnp.int32), lengths])
    )
    swap = ring(2, 1)

    q5 = queries.reshape(NX, 4, 128, 256)

    def q_spec(flip_z, flip_c):
        def index(i, s):
            z = 1 - s[ZH] if flip_z else s[ZH]
            core = 1 - s[C] if flip_c else s[C]
            return (0, z * 2 + core, 0, 0)

        return pl.BlockSpec((NX, 1, 128, 256), index)

    def w_spec(k, other):
        return pl.BlockSpec(
            (256, blk), lambda i, s: (0, (1 - s[G] if other else s[G]) * 4 + (s[D] + k) % 4)
        )

    q_shape = ((NX, 128, 256), BF)
    w_shapes = [((256, len(ks) * blk), BF) for ks in STAGES]
    p_core, p_z0, p_z1, *w_sent = call(
        pick_kernel,
        scalars,
        [
            (q5, q_spec(False, True)),
            (q5, q_spec(True, False)),
            (q5, q_spec(True, True)),
            *[(out_weight, w_spec(k, True)) for ks in STAGES for k in ks],
        ],
        [q_shape, q_shape, q_shape, *w_shapes],
        "pick",
    )
    q_core = lax.ppermute(p_core, "core", swap)
    q_z0 = lax.ppermute(p_z0, ("grp", "zh"), WRAP)
    q_z1 = lax.ppermute(p_z1, ("grp", "zh", "core"), WRAP_CORE)
    w_half = jnp.where(g == 0, out_weight[:, :half], out_weight[:, half:])
    w_core = lax.ppermute(w_half, "core", swap)

    hidden, _ = barrier((student_hidden[0], p_core))
    hidden = hidden.astype(F32)
    inverse_rms = lax.rsqrt(jnp.mean(hidden * hidden, axis=-1, keepdims=True) + 1e-06)
    unit_rows = hidden * inverse_rms
    scaled_rows = unit_rows * norm_gain
    normed = scaled_rows.astype(BF)
    scalars.after(normed)
    normed = lax.all_gather(normed, "dp", axis=0, tiled=True)

    def attend(q0, spec0, q1, name):
        return call(
            attend_kernel,
            scalars,
            [
                (q0, spec0),
                (q1, whole((NX, 128, 256))),
                (keys[0], pl.BlockSpec((2048, HD), lambda i, s: (0, s[X]))),
                (values[0], pl.BlockSpec((2048, HD), lambda i, s: (0, s[X]))),
            ],
            [((512, 512), BF)],
            name,
            scratch=[pltpu.VMEM((2048, 2 * HD), BF)],
            mib=40,
        )[0]

    ctx_a = attend(q5, q_spec(False, False), q_core, "attend_chip")
    w_z = [lax.ppermute(w, ("grp", "zh"), WRAP) for w in w_sent]
    ctx_b = attend(q_z0, whole((NX, 128, 256)), q_z1, "attend_next")
    piece = ((128, blk), BF)
    projected = []
    for stage, ks in enumerate(STAGES):
        n = len(ks)
        w_mine, _ = barrier((w_z[stage], scalars.value))
        if stage:
            w_mine, _ = barrier((w_mine, projected[-1][1][1]))
        w_zc = lax.ppermute(w_mine, "core", swap)
        own, *outs = call(
            project_kernel,
            scalars,
            [
                (ctx_a, whole((512, 512))),
                (ctx_b, whole((512, 512))),
                (w_mine, whole((256, n * blk))),
                (w_zc, whole((256, n * blk))),
                *[(out_weight, w_spec(k, False)) for k in ks],
                *[
                    (w_core, pl.BlockSpec((256, blk), lambda i, s, k=k: (0, (s[D] + k) % 4)))
                    for k in ks
                ],
            ],
            [((128, n * blk), F32)] + [((128, n * blk), BF)] * 3,
            f"project_{stage}",
            scratch=[pltpu.VMEM((512, n * blk), F32)],
        )
        projected.append((own, {j: lax.ppermute(outs[j - 1], "x", ring(NX, j)) for j in (2, 1, 3)}))

    normed, _ = barrier((normed, own))
    predicted = jnp.dot(normed, projection, preferred_element_type=F32)
    scalars.after(predicted)

    done_of, there_of = {}, {}
    gp_of, back_of = {}, {}
    gain_part = jnp.zeros((1, D_S), F32)
    squared = jnp.zeros((), F32)

    def finish(stage):
        ks = STAGES[stage]
        n = len(ks)
        own, got = projected[stage]
        sums = [
            (own, whole((128, n * blk))),
            *[(got[j], whole((128, n * blk))) for j in (1, 2, 3)],
            *[
                (
                    residual[0],
                    pl.BlockSpec((128, blk), lambda i, s, k=k: (0, s[G] * 4 + (s[D] + k) % 4)),
                )
                for k in ks
            ],
        ]
        outs = [piece] * n
        if stage == len(STAGES) - 1:
            sums += [(done_of[k], whole((128, blk))) for k in ORDER[:-n]]
            outs = outs + [((128, half), BF)]
        done = call(finish_kernel, scalars, sums, outs, f"finish_{stage}")
        for k, a in zip(ks, done):
            done_of[k] = a
            there_of[k] = a if k == 0 else lax.ppermute(a, "dp", ring(4, k))
        return done[-1]

    def compare(stage):
        ks = STAGES[stage]
        n = len(ks)

        def kernel(*refs):
            compare_kernel(ks, *refs)

        outs = call(
            kernel,
            scalars,
            [
                (predicted, whole((512, blk))),
                (normed, whole((512, D_S))),
                (projection, whole((D_S, blk))),
                *[(there_of[k], whole((128, blk))) for k in ks],
            ],
            [piece] * n
            + [((128, D_S), F32 if k == 0 else BF) for k in ks]
            + [((1, D_S), F32), ((1, blk), F32)],
            f"compare_{stage}",
            scratch=[pltpu.VMEM((n * 128, blk), BF)],
        )
        for k, gp, back in zip(ks, outs[:n], outs[n:]):
            gp_of[k] = gp
            back_of[k] = back if k == 0 else lax.ppermute(back, "dp", ring(4, 4 - k))
        return outs[-2], outs[-1]

    for step in STEPS:
        if step < 10:
            target = finish(step)
        else:
            gain, loss = compare(step - 10)
            gain_part = gain_part + gain
            squared = squared + jnp.sum(loss)

    live_count = jnp.sum(lengths).astype(F32)
    part = (NX, 2, rows, blk)
    sent, kept = call(
        gproj_kernel,
        scalars,
        [(normed, whole((512, D_S)))] + [(gp_of[k], whole((128, blk))) for k in (2, 1, 3, 0)],
        [(part, BF), (part, F32)],
        "gproj",
        scratch=[pltpu.VMEM((512, blk), BF)],
    )
    small = jnp.concatenate([gain_part[0] / norm_gain, jnp.full((128,), squared)]).reshape(-1, 128)
    recv = lax.ppermute(sent, "core", swap)
    small, _ = barrier((small, sent))
    small = small + lax.ppermute(small, "core", swap)
    own, *outs = call(
        gproj_add_kernel,
        scalars,
        [(kept, whole(part)), (recv, whole(part))],
        [(part[1:], F32)] + [(part[1:], BF)] * 3,
        "gproj_add",
    )
    got = {j: lax.ppermute(outs[j - 1], "x", ring(NX, j)) for j in (2, 1, 3)}
    small, _ = barrier((small, own))
    small = sum([lax.ppermute(small, ("grp", "zh"), ring(NZ, j)) for j in range(1, 4)], small)

    scalars.after(got[1])
    width = D_S // 2
    sent, kept, inner = call(
        combine_kernel,
        scalars,
        [(back_of[k], whole((128, D_S))) for k in range(4)]
        + [(scaled_rows, whole((128, D_S)))],
        [((128, width), BF), ((128, width), F32), ((128, 1), F32)],
        "combine",
    )
    inner = inner.reshape(1, 128)
    inner_recv = lax.ppermute(inner, "grp", swap)
    half_recv = lax.ppermute(sent, "grp", swap)
    small, _ = barrier((small, sent))
    small = sum([lax.ppermute(small, "dp", ring(4, j)) for j in range(1, 4)], small)
    scalars.after(small)

    gsent, gkept = call(
        gproj_sum_kernel,
        scalars,
        [(own, whole(part[1:]))] + [(got[j], whole(part[1:])) for j in (1, 2, 3)],
        [((rows, blk), BF), ((rows, blk), F32)],
        "gproj_sum",
    )
    small, _ = barrier((small, gsent))
    gsent = lax.ppermute(gsent, "zh", swap)
    small = sum([lax.ppermute(small, "x", ring(NX, j)) for j in range(1, 4)], small)
    small = small.reshape(-1)
    gkept, kept = barrier((gkept, kept))
    inner = (inner + inner_recv).reshape(128, 1)
    grad_half = kept + half_recv.astype(F32)
    gain_half = lax.dynamic_slice_in_dim(norm_gain, g * width, width, 0)
    unit_half = jnp.where(g == 0, unit_rows[:, :width], unit_rows[:, width:])
    grad_hidden = inverse_rms * (grad_half * gain_half - unit_half * (inner / D_S))
    grad_proj = (gkept + gsent.astype(F32)) / live_count
    distill_loss = small[D_S] / (live_count * D_T)
    grad_gain = lax.dynamic_slice_in_dim(small, g * (D_S // 2), D_S // 2, 0) / live_count
    return (target[None], distill_loss, grad_proj, grad_gain, grad_hidden[None])


def solution(mesh):
    fine = Mesh(mesh.devices.reshape(2, 4, 4, 2, 2), ("grp", "dp", "x", "zh", "core"))
    in_specs = (
        P("dp", None, MP),
        P("dp", None, None),
        P("dp", None, None),
        P(MP, None),
        P("dp", MP, None),
        P("dp", MP, None),
        P(),
        P(None, ("grp", "dp")),
        P(),
    )
    out_specs = (P("dp", MP, "grp"), P(), P(MP, ("grp", "dp")), P("grp"), P("dp", MP, "grp"))
    return jax.shard_map(body, mesh=fine, in_specs=in_specs, out_specs=out_specs, check_vma=False)
```

```python
import math

import jax
import jax.numpy as jnp
from jax import lax
from jax.experimental import pallas as pl
from jax.experimental.pallas import tpu as pltpu
from jax.sharding import Mesh
from jax.sharding import PartitionSpec as P

D_T = 5120
D_S = 2560
HD = 128
HQ = 32
KVH = 4

BF = jnp.bfloat16
F32 = jnp.float32
NX = 4
NZ = 4
MP = ("x", "zh", "core")


def ring(n, k):
    return [(i, (i + k) % n) for i in range(n)]


WRAP = [(g * 2 + z, (1 - g) * 2 + (1 - z)) for g in range(2) for z in range(2)]
MIB = 32
COST = 1


def block_of(stage, core):
    return 2 + core if stage == 0 else 1 - core


def to_owner(stage, cross):
    return [
        (d * 2 + c, (d + block_of(stage, c)) % 4 * 2 + (1 - c if cross else c))
        for d in range(4)
        for c in range(2)
    ]


def whole(shape):
    return pl.BlockSpec(shape, lambda i, s: (0,) * len(shape))


def call(kernel, scalars, ins, outs, name, scratch=(), mib=MIB):
    outs = pl.pallas_call(
        kernel,
        out_shape=[jax.ShapeDtypeStruct(shape, t) for shape, t in outs],
        grid_spec=pltpu.PrefetchScalarGridSpec(
            num_scalar_prefetch=1,
            grid=(1,),
            in_specs=[spec for _, spec in ins],
            out_specs=[whole(shape) for shape, _ in outs],
            scratch_shapes=list(scratch),
        ),
        compiler_params=pltpu.CompilerParams(vmem_limit_bytes=mib * 1024 * 1024),
        cost_estimate=pl.CostEstimate(flops=COST, bytes_accessed=COST, transcendentals=0),
        name=name,
    )(scalars.value, *[a for a, _ in ins])
    scalars.after(outs[0])
    return outs


class Ordered:
    def __init__(self, value):
        self.value = value

    def after(self, array):
        self.value, _ = lax.optimization_barrier((self.value, array))


X, ZC, G, D, ZH, C, FIRST, LENGTHS = range(8)


def pick_kernel(s, q, w0, w1, w2, w3, res0, res1, q_out, w_out, res_out):
    q_out[...] = q[...]
    for i, w in enumerate((w0, w1, w2, w3)):
        w_out[:, i * 640 : i * 640 + 640] = w[...]
    res_out[:, :640] = res0[...]
    res_out[:, 640:] = res1[...]


def pick_weights_kernel(s, own0, own1, other, out0, out1):
    for i, (own, out) in enumerate(((own0, out0), (own1, out1))):
        out[:256] = own[...]
        out[256:] = other[:, i * 640 : i * 640 + 640]


def attend_kernel(s, q_ref, k_ref, v_ref, out_ref, vext):
    vext[:, :HD] = v_ref[...]
    vext[:, HD:] = jnp.ones((v_ref.shape[0], HD), BF)
    scale = HD ** (-0.5) * math.log2(math.e)
    rows = lax.broadcasted_iota(jnp.int32, (256, 512), 0) % 128
    cols = lax.broadcasted_iota(jnp.int32, (256, 512), 1)
    behind = cols - rows
    for part in range(NX):
        length = 512 * (part + 1)
        for block in range(2):
            q = q_ref[part, block]
            q = jnp.concatenate([q[:, :HD], q[:, HD:]], axis=0)
            scores = lax.dot_general(
                q, k_ref[:length, :], (((1,), (1,)), ((), ())), preferred_element_type=F32
            )
            allowed = behind <= (s[ZH] * 2 + block) * 128
            last = jnp.where(allowed, scores[:, length - 512 :], -1e30)
            if part:
                scores = jnp.concatenate([scores[:, : length - 512], last], axis=1)
            else:
                scores = last
            top = jnp.max(scores, axis=-1, keepdims=True)
            probs = jnp.exp2((scores - top) * scale).astype(BF)
            mixed = jnp.dot(probs, vext[:length, :], preferred_element_type=F32)
            mixed = (mixed[:, :HD] / mixed[:, HD:]).astype(BF)
            at = (block * NX + part) * 128
            out_ref[at : at + 128, :HD] = mixed[:128]
            out_ref[at : at + 128, HD:] = mixed[128:]


def project_kernel(s, ctx_a, ctx_ac, ctx_b, ctx_bc, w_a, w_ac, w_z, own, o1, o2, o3, total):
    def dot(a, b):
        return jnp.dot(a[...], b, preferred_element_type=F32)

    total[...] = (
        dot(ctx_a, w_a[...])
        + dot(ctx_ac, w_ac[...])
        + dot(ctx_b, w_z[:256])
        + dot(ctx_bc, w_z[256:])
    )
    for j, out in enumerate((own, o1, o2, o3)):
        for block in range(2):
            at = pl.multiple_of((block * NX + (s[X] + j) % NX) * 128, 128)
            out[block] = total[pl.ds(at, 128), :].astype(out.dtype)


def finish_kernel(s, own, r1, r2, r3, res, res_other, *refs):
    def rows(at):
        parts = own[at] + r1[at].astype(F32) + r2[at].astype(F32) + r3[at].astype(F32)
        return parts

    same, cross = refs[-2], refs[-1]
    same[...] = (res[...].astype(F32) + rows(s[C])).astype(BF)
    cross[...] = (res_other[...].astype(F32) + rows(1 - s[C])).astype(BF)


def assemble_kernel(s, same0, same1, got0, got1, target):
    for piece, stage, core in (
        (same0, 0, s[C]),
        (same1, 1, s[C]),
        (got0, 0, 1 - s[C]),
        (got1, 1, 1 - s[C]),
    ):
        at = pl.multiple_of(((s[D] + block_of(stage, core)) % 4) * 640, 128)
        target[:, pl.ds(at, 640)] = piece[...]


def three_parts(value):
    high = value.astype(BF)
    rest = value - high.astype(F32)
    middle = rest.astype(BF)
    low = rest - middle.astype(F32)
    lane = lax.broadcasted_iota(jnp.int32, (value.shape[0], 128), 1)
    wide = jnp.where(lane == 0, high.astype(F32), jnp.where(lane == 1, middle.astype(F32), 0.0))
    return jnp.where(lane == 2, low, wide).astype(BF)


def compare_kernel(s, pred, normed, proj, sm0, cr0, sm1, cr1, gp, gain, loss, *refs):
    first_of = refs[:3]
    last_of = refs[3:6]
    own_first, own_last, own_inner, grad, inner = refs[6:]
    square = jnp.zeros((1, 640), F32)
    for got, stage, core in (
        (sm0, 0, s[C]),
        (cr0, 0, 1 - s[C]),
        (sm1, 1, s[C]),
        (cr1, 1, 1 - s[C]),
    ):
        seq = (s[D] + 4 - block_of(stage, core)) % 4
        at = pl.multiple_of(seq * 128, 128)
        live = lax.broadcasted_iota(jnp.int32, (128, 640), 0) < s[LENGTHS + seq] - s[FIRST]
        here = pred[pl.ds(at, 128), :]
        diff = jnp.where(live, here - got[...].astype(F32), 0.0)
        square = square + jnp.sum(diff * diff, axis=0, keepdims=True)
        rounded = diff.astype(BF)
        gp[pl.ds(at, 128), :] = rounded
        inner[pl.ds(at, 128), :] = jnp.sum(rounded.astype(F32) * here, axis=-1, keepdims=True)
    loss[...] = square
    for far, outs, own in ((1, first_of, own_first), (0, last_of, own_last)):
        for part in range(2):
            half = s[G] if far == 0 else 1 - s[G]
            base = pl.multiple_of(half * 1280 + part * 640, 128)
            cols = slice(part * 640, part * 640 + 640)
            grad[...] = lax.dot_general(
                gp[...],
                proj[pl.ds(base, 640), :],
                (((1,), (1,)), ((), ())),
                preferred_element_type=F32,
            )
            gain[:, pl.ds(base, 640)] = jnp.sum(
                grad[...] * normed[:, pl.ds(base, 640)].astype(F32), axis=0, keepdims=True
            )
            for k in range(4):
                at = pl.multiple_of(((s[D] + 4 - k) % 4) * 128, 128)
                rows = grad[pl.ds(at, 128), :]
                if k == 0:
                    own[:, cols] = rows
                else:
                    outs[k - 1][:, cols] = rows.astype(BF)
    for k in range(4):
        at = pl.multiple_of(((s[D] + 4 - k) % 4) * 128, 128)
        if k == 0:
            own_inner[...] = inner[pl.ds(at, 128), :]
        else:
            first_of[k - 1][:, 1280:] = three_parts(inner[pl.ds(at, 128), :])


def added(own, parts, inner=None):
    total, inner_sum = own[...], None if inner is None else inner[...]
    for r in parts:
        total = total + r[:, :1280].astype(F32)
        if inner is not None:
            inner_sum = inner_sum + jnp.sum(r[:, 1280:].astype(F32), axis=-1, keepdims=True)
    return total, inner_sum


def combine_kernel(s, own, own_inner, r1, r2, r3, sent, inner):
    total, inner_sum = added(own, (r1, r2, r3), own_inner)
    sent[:, :1280] = total.astype(BF)
    sent[:, 1280:] = three_parts(inner_sum)
    inner[...] = inner_sum


def hidden_kernel(s, own, r1, r2, r3, inner, got, hidden, inverse_rms, gain, out):
    total, _ = added(own, (r1, r2, r3))
    inner_sum = inner[...] + jnp.sum(got[:, 1280:].astype(F32), axis=-1, keepdims=True)
    grad = total + got[:, :1280].astype(F32)
    scale = inverse_rms[...]
    unit = hidden[...].astype(F32) * scale
    out[...] = scale * (grad * gain[...] - unit * (inner_sum / D_S))


def gproj_kernel(s, normed, gp, sent, kept):
    first = s[C] == 0
    for part in range(NX):
        total = lax.dot_general(
            normed[:, part * 640 : part * 640 + 640],
            gp[...],
            (((0,), (0,)), ((), ())),
            preferred_element_type=F32,
        )
        for z in range(2):
            low = total[z * 320 : z * 320 + 160]
            high = total[z * 320 + 160 : z * 320 + 320]
            sent[part, z] = jnp.where(first, high, low).astype(BF)
            kept[part, z] = jnp.where(first, low, high)


def gproj_add_kernel(s, kept, recv, own, o1, o2, o3):
    for j, out in enumerate((own, o1, o2, o3)):
        at = (s[X] + j) % NX
        out[...] = (kept[at] + recv[at].astype(F32)).astype(out.dtype)


def gproj_sum_kernel(s, own, r1, r2, r3, sent, kept):
    z = s[ZH]

    def total(at):
        return own[at] + r1[at].astype(F32) + r2[at].astype(F32) + r3[at].astype(F32)

    sent[...] = total(1 - z).astype(BF)
    kept[...] = total(z)


def sum_over(array, axis, n):
    got = [lax.ppermute(array, axis, ring(n, j)) for j in range(1, n)]
    got = lax.optimization_barrier(got)
    return sum(got, array)


def body(
    queries, keys, values, out_weight, residual, student_hidden, norm_gain, projection, lengths
):
    g, d = lax.axis_index("grp"), lax.axis_index("dp")
    x, zh, c = lax.axis_index("x"), lax.axis_index("zh"), lax.axis_index("core")
    zc = zh * 2 + c
    m = x * 4 + zc
    half = D_T // 2
    blk = D_T // 8
    rows = D_S // 16
    width = D_S // 2
    barrier = lax.optimization_barrier
    scalars = Ordered(
        jnp.concatenate([jnp.stack([x, zc, g, d, zh, c, m * 128]).astype(jnp.int32), lengths])
    )
    swap = ring(2, 1)
    stages = (0, 1)

    def column(stage, near, mine, n):
        def index(i, s):
            core = s[C] if mine else 1 - s[C]
            side = s[G] if near else 1 - s[G]
            return (0, side * 4 + (s[D] + block_of(stage, core)) % 4)

        return pl.BlockSpec((n, blk), index)

    q5 = queries.reshape(NX, 4, 128, 256)
    q_block = (NX, 2, 128, 256)
    along_z, w_out, res_out = call(
        pick_kernel,
        scalars,
        [
            (q5, pl.BlockSpec(q_block, lambda i, s: (0, 1 - s[ZH], 0, 0))),
            *[(out_weight, column(st, near, False, 256)) for near in (False, True) for st in stages],
            *[(residual[0], column(st, True, False, 128)) for st in stages],
        ],
        [(q_block, BF), ((256, 4 * blk), BF), ((128, 2 * blk), BF)],
        "pick",
    )
    along_z = lax.ppermute(along_z, ("grp", "zh"), WRAP)
    w_other = lax.ppermute(w_out, "core", swap)
    res_other = lax.ppermute(res_out, "core", swap)

    hidden, _ = barrier((student_hidden[0], w_out))
    hidden = hidden.astype(F32)
    inverse_rms = lax.rsqrt(jnp.mean(hidden * hidden, axis=-1, keepdims=True) + 1e-06)
    normed = (hidden * inverse_rms * norm_gain).astype(BF)
    scalars.after(normed)
    normed = lax.all_gather(normed, "dp", axis=0, tiled=True)

    def attend(q, spec, name):
        return call(
            attend_kernel,
            scalars,
            [
                (q, spec),
                (keys[0], pl.BlockSpec((2048, HD), lambda i, s: (0, s[X]))),
                (values[0], pl.BlockSpec((2048, HD), lambda i, s: (0, s[X]))),
            ],
            [((1024, 256), BF)],
            name,
            scratch=[pltpu.VMEM((2048, 2 * HD), BF)],
            mib=40,
        )[0]

    ctx_a = attend(q5, pl.BlockSpec(q_block, lambda i, s: (0, s[ZH], 0, 0)), "attend_chip")
    w_z = call(
        pick_weights_kernel,
        scalars,
        [
            *[(out_weight, column(st, False, True, 256)) for st in stages],
            (w_other, pl.BlockSpec((256, 2 * blk), lambda i, s: (0, 0))),
        ],
        [((512, blk), BF)] * 2,
        "pick_weights",
    )
    w_z = [lax.ppermute(w, ("grp", "zh"), WRAP) for w in w_z]
    ctx_ac = lax.ppermute(ctx_a, "core", swap)
    along_z, _ = barrier((along_z, ctx_a))
    ctx_b = attend(along_z, whole(q_block), "attend_next")
    ctx_bc = lax.ppermute(ctx_b, "core", swap)

    projected = []
    for st in stages:
        own, *outs = call(
            project_kernel,
            scalars,
            [
                *[(ctx, whole((1024, 256))) for ctx in (ctx_a, ctx_ac, ctx_b, ctx_bc)],
                (out_weight, column(st, True, True, 256)),
                (w_other, pl.BlockSpec((256, blk), lambda i, s, st=st: (0, 2 + st))),
                (w_z[st], whole((512, blk))),
            ],
            [((2, 128, blk), F32)] + [((2, 128, blk), BF)] * 3,
            f"project_{st}",
            scratch=[pltpu.VMEM((1024, blk), F32)],
        )
        if st == 0:
            normed, _ = barrier((normed, own))
            predicted = jnp.dot(normed, projection, preferred_element_type=F32)
            scalars.after(predicted)
        projected.append((own, {j: lax.ppermute(outs[j - 1], "x", ring(NX, j)) for j in (2, 1, 3)}))

    compared, same, cross = [], [], []
    for st in stages:
        own, got = projected[st]
        done_same, done_cross = call(
            finish_kernel,
            scalars,
            [
                (own, whole((2, 128, blk))),
                *[(got[j], whole((2, 128, blk))) for j in (1, 2, 3)],
                (residual[0], column(st, True, True, 128)),
                (res_other, pl.BlockSpec((128, blk), lambda i, s, st=st: (0, st))),
            ],
            [((128, blk), BF)] * 2,
            f"finish_{st}",
        )
        same.append(done_same)
        cross.append(done_cross)
        compared.append(lax.ppermute(done_same, ("dp", "core"), to_owner(st, False)))
        compared.append(lax.ppermute(done_cross, ("dp", "core"), to_owner(st, True)))

    first_shape, last_shape = (128, width + 128), (128, width)
    gp, gain, loss, *backs, own_first, own_last, own_inner = call(
        compare_kernel,
        scalars,
        [
            (predicted, whole((512, blk))),
            (normed, whole((512, D_S))),
            (projection, whole((D_S, blk))),
            *[(a, whole((128, blk))) for a in compared],
        ],
        [((512, blk), BF), ((1, D_S), F32), ((1, blk), F32)]
        + [(first_shape, BF)] * 3
        + [(last_shape, BF)] * 3
        + [(last_shape, F32), (last_shape, F32), ((128, 1), F32)],
        "compare",
        scratch=[pltpu.VMEM((512, blk), F32), pltpu.VMEM((512, 1), F32)],
    )
    back_first = [lax.ppermute(backs[k - 1], "dp", ring(4, 4 - k)) for k in (1, 2, 3)]

    live_count = jnp.sum(lengths).astype(F32)
    part = (NX, 2, rows, blk)
    sent, kept = call(
        gproj_kernel,
        scalars,
        [(normed, whole((512, D_S))), (gp, whole((512, blk)))],
        [(part, BF), (part, F32)],
        "gproj",
    )
    recv = lax.ppermute(sent, "core", swap)
    small = jnp.concatenate([gain[0] / norm_gain, jnp.full((128,), jnp.sum(loss))]).reshape(-1, 128)
    small, _ = barrier((small, sent))
    small = sum_over(small, "dp", 4)
    own, *outs = call(
        gproj_add_kernel,
        scalars,
        [(kept, whole(part)), (recv, whole(part))],
        [(part[1:], F32)] + [(part[1:], BF)] * 3,
        "gproj_add",
    )
    got = {j: lax.ppermute(outs[j - 1], "x", ring(NX, j)) for j in (2, 1, 3)}
    *lasts, small = barrier((*backs[3:6], small))
    back_last = [lax.ppermute(lasts[k - 1], "dp", ring(4, 4 - k)) for k in (1, 2, 3)]
    small = small + lax.ppermute(small, "core", swap)
    small = sum_over(small, ("grp", "zh"), NZ)

    sent, inner = call(
        combine_kernel,
        scalars,
        [
            (own_first, whole(last_shape)),
            (own_inner, whole((128, 1))),
            *[(r, whole(first_shape)) for r in back_first],
        ],
        [(first_shape, BF), ((128, 1), F32)],
        "combine",
    )
    half_recv = lax.ppermute(sent, "grp", swap)
    cross = [lax.ppermute(a, "core", swap) for a in barrier((*cross, sent))[:2]]
    (target,) = call(
        assemble_kernel,
        scalars,
        [(a, whole((128, blk))) for a in (*same, *cross)],
        [((128, half), BF)],
        "assemble",
    )
    gsent, gkept = call(
        gproj_sum_kernel,
        scalars,
        [(own, whole(part[1:]))] + [(got[j], whole(part[1:])) for j in (1, 2, 3)],
        [((rows, blk), BF), ((rows, blk), F32)],
        "gproj_sum",
    )
    small, _ = barrier((small, gsent))
    gsent = lax.ppermute(gsent, "zh", swap)
    small = sum_over(small, "x", NX).reshape(-1)
    scalars.after(small)
    (grad_hidden,) = call(
        hidden_kernel,
        scalars,
        [
            (own_last, whole(last_shape)),
            *[(r, whole(last_shape)) for r in back_last],
            (inner, whole((128, 1))),
            (half_recv, whole(first_shape)),
            (student_hidden[0], pl.BlockSpec((128, width), lambda i, s: (0, s[G]))),
            (inverse_rms, whole((128, 1))),
            (norm_gain.reshape(1, D_S), pl.BlockSpec((1, width), lambda i, s: (0, s[G]))),
        ],
        [(last_shape, F32)],
        "hidden",
    )
    grad_proj = (gkept + gsent.astype(F32)) / live_count
    distill_loss = small[D_S] / (live_count * D_T)
    grad_gain = lax.dynamic_slice_in_dim(small, g * width, width, 0) / live_count
    return (target[None], distill_loss, grad_proj, grad_gain, grad_hidden[None])


def solution(mesh):
    fine = Mesh(mesh.devices.reshape(2, 4, 4, 2, 2), ("grp", "dp", "x", "zh", "core"))
    in_specs = (
        P("dp", None, MP),
        P("dp", None, None),
        P("dp", None, None),
        P(MP, None),
        P("dp", MP, None),
        P("dp", MP, None),
        P(),
        P(None, ("grp", "dp")),
        P(),
    )
    out_specs = (P("dp", MP, "grp"), P(), P(MP, ("grp", "dp")), P("grp"), P("dp", MP, "grp"))
    return jax.shard_map(body, mesh=fine, in_specs=in_specs, out_specs=out_specs, check_vma=False)
```

```python
import math

import jax
import jax.numpy as jnp
from jax import lax
from jax.experimental import pallas as pl
from jax.experimental.pallas import tpu as pltpu
from jax.sharding import Mesh
from jax.sharding import PartitionSpec as P

D_T = 5120
D_S = 2560
HD = 128
HQ = 32
KVH = 4

BF = jnp.bfloat16
F32 = jnp.float32
NX = 4
NZ = 4
MP = ("x", "zh", "core")


def ring(n, k):
    return [(i, (i + k) % n) for i in range(n)]


WRAP = [(g * 2 + z, (1 - g) * 2 + (1 - z)) for g in range(2) for z in range(2)]
MIB = 32
COST = 1


def block_of(stage, core):
    return 2 + core if stage == 0 else 1 - core


def to_owner(stage, cross):
    return [
        (d * 2 + c, (d + block_of(stage, c)) % 4 * 2 + (1 - c if cross else c))
        for d in range(4)
        for c in range(2)
    ]


def whole(shape):
    return pl.BlockSpec(shape, lambda i, s: (0,) * len(shape))


def call(kernel, scalars, ins, outs, name, scratch=(), mib=MIB, pinned=(), steps=1):
    outs = pl.pallas_call(
        kernel,
        out_shape=[
            pltpu.HBM(o[0], o[1]) if len(o) == 3 else jax.ShapeDtypeStruct(*o) for o in outs
        ],
        grid_spec=pltpu.PrefetchScalarGridSpec(
            num_scalar_prefetch=1,
            grid=(steps,),
            in_specs=[spec for _, spec in ins],
            out_specs=[whole(o[0]) for o in outs],
            scratch_shapes=list(scratch),
        ),
        compiler_params=pltpu.CompilerParams(vmem_limit_bytes=mib * 1024 * 1024),
        cost_estimate=pl.CostEstimate(flops=COST, bytes_accessed=COST, transcendentals=0),
        name=name,
    )(scalars.value, *[
            pltpu.with_memory_space_constraint(a, pltpu.HBM) if i in pinned else a
            for i, (a, _) in enumerate(ins)
        ])
    scalars.after(outs[0])
    return outs


class Ordered:
    def __init__(self, value):
        self.value = value

    def after(self, array):
        self.value, _ = lax.optimization_barrier((self.value, array))


X, ZC, G, D, ZH, C, FIRST, LENGTHS = range(8)


def column_block(s, stage, near, mine):
    core = s[C] if mine else 1 - s[C]
    side = s[G] if near else 1 - s[G]
    return side * 4 + (s[D] + block_of(stage, core)) % 4


def pick_kernel(s, q, w0, w1, w2, w3, res0, res1, q_out, w_out, res_out):
    q_out[...] = q[...]
    for i, w in enumerate((w0, w1, w2, w3)):
        w_out[:, i * 640 : i * 640 + 640] = w[...]
    res_out[:, :640] = res0[...]
    res_out[:, 640:] = res1[...]


def pick_weights_kernel(s, own0, own1, other, out0, out1):
    for i, (own, out) in enumerate(((own0, out0), (own1, out1))):
        out[:256] = own[...]
        out[256:] = other[:, i * 640 : i * 640 + 640]


def attend_kernel(s, q_ref, k_ref, v_ref, out_ref, vext):
    vext[:, :HD] = v_ref[...]
    vext[:, HD:] = jnp.ones((v_ref.shape[0], HD), BF)
    scale = HD ** (-0.5) * math.log2(math.e)
    rows = lax.broadcasted_iota(jnp.int32, (256, 512), 0) % 128
    cols = lax.broadcasted_iota(jnp.int32, (256, 512), 1)
    behind = cols - rows
    for part in range(NX):
        length = 512 * (part + 1)
        for block in range(2):
            q = q_ref[part, block]
            q = jnp.concatenate([q[:, :HD], q[:, HD:]], axis=0)
            scores = lax.dot_general(
                q, k_ref[:length, :], (((1,), (1,)), ((), ())), preferred_element_type=F32
            )
            allowed = behind <= (s[ZH] * 2 + block) * 128
            last = jnp.where(allowed, scores[:, length - 512 :], -1e30)
            if part:
                scores = jnp.concatenate([scores[:, : length - 512], last], axis=1)
            else:
                scores = last
            top = jnp.max(scores, axis=-1, keepdims=True)
            probs = jnp.exp2((scores - top) * scale).astype(BF)
            mixed = jnp.dot(probs, vext[:length, :], preferred_element_type=F32)
            mixed = (mixed[:, :HD] / mixed[:, HD:]).astype(BF)
            at = (block * NX + part) * 128
            out_ref[at : at + 128, :HD] = mixed[:128]
            out_ref[at : at + 128, HD:] = mixed[128:]


def project_kernel(s, ctx_a, ctx_ac, ctx_b, ctx_bc, w_a, w_ac, w_z, own, o1, o2, o3, total):
    def dot(a, b):
        return jnp.dot(a[...], b, preferred_element_type=F32)

    total[...] = (
        dot(ctx_a, w_a[...])
        + dot(ctx_ac, w_ac[...])
        + dot(ctx_b, w_z[:256])
        + dot(ctx_bc, w_z[256:])
    )
    for j, out in enumerate((own, o1, o2, o3)):
        for block in range(2):
            at = pl.multiple_of((block * NX + (s[X] + j) % NX) * 128, 128)
            out[block] = total[pl.ds(at, 128), :].astype(out.dtype)


def finish_kernel(s, own, r1, r2, r3, res, res_other, *refs):
    def rows(at):
        parts = own[at] + r1[at].astype(F32) + r2[at].astype(F32) + r3[at].astype(F32)
        return parts

    same, cross = refs[-2], refs[-1]
    same[...] = (res[...].astype(F32) + rows(s[C])).astype(BF)
    cross[...] = (res_other[...].astype(F32) + rows(1 - s[C])).astype(BF)


def assemble_kernel(s, same0, same1, got0, got1, target):
    for piece, stage, core in (
        (same0, 0, s[C]),
        (same1, 1, s[C]),
        (got0, 0, 1 - s[C]),
        (got1, 1, 1 - s[C]),
    ):
        at = pl.multiple_of(((s[D] + block_of(stage, core)) % 4) * 640, 128)
        target[:, pl.ds(at, 640)] = piece[...]


def compare_kernel(s, pred, normed, proj, sm0, cr0, sm1, cr1, gp, back, small, inner):
    square = jnp.zeros((1, 640), F32)
    for got, stage, core in (
        (sm0, 0, s[C]),
        (cr0, 0, 1 - s[C]),
        (sm1, 1, s[C]),
        (cr1, 1, 1 - s[C]),
    ):
        seq = (s[D] + 4 - block_of(stage, core)) % 4
        at = pl.multiple_of(seq * 128, 128)
        live = lax.broadcasted_iota(jnp.int32, (128, 640), 0) < s[LENGTHS + seq] - s[FIRST]
        here = pred[pl.ds(at, 128), :]
        diff = jnp.where(live, here - got[...].astype(F32), 0.0)
        square = square + jnp.sum(diff * diff, axis=0, keepdims=True)
        rounded = diff.astype(BF)
        gp[pl.ds(at, 128), :] = rounded
        inner[pl.ds(at, 128), :] = jnp.sum(rounded.astype(F32) * here, axis=-1, keepdims=True)
    small[...] = jnp.zeros((32, 128), F32)
    small[20:21, :] = jnp.broadcast_to(jnp.sum(square, axis=-1, keepdims=True), (1, 128))
    turned = jnp.broadcast_to(inner[...], (512, 128)).T
    for i in range(4):
        small[21 + i : 22 + i, :] = turned[:1, i * 128 : i * 128 + 128]
    for part in range(4):
        cols = slice(part * 640, part * 640 + 640)
        grad = lax.dot_general(
            gp[...], proj[cols, :], (((1,), (1,)), ((), ())), preferred_element_type=F32
        )
        back[part // 2, :, (part % 2) * 640 : (part % 2) * 640 + 640] = grad.astype(BF)
        gain = jnp.sum(grad * normed[:, cols].astype(F32), axis=0, keepdims=True)
        for i in range(5):
            small[part * 5 + i : part * 5 + i + 1, :] = gain[:, i * 128 : i * 128 + 128]


def hidden_kernel(s, grad, inner, hidden, inverse_rms, norm_gain, out):
    scale = inverse_rms[...]
    unit = hidden[...].astype(F32) * scale
    out[...] = scale * (grad[...].astype(F32) * norm_gain[...] - unit * (inner[...] / D_S))


def gproj_kernel(s, normed, gp, sent, kept):
    first = s[C] == 0
    for part in range(NX):
        total = lax.dot_general(
            normed[:, part * 640 : part * 640 + 640],
            gp[...],
            (((0,), (0,)), ((), ())),
            preferred_element_type=F32,
        )
        for z in range(2):
            low = total[z * 320 : z * 320 + 160]
            high = total[z * 320 + 160 : z * 320 + 320]
            sent[part, z] = jnp.where(first, high, low).astype(BF)
            kept[part, z] = jnp.where(first, low, high)


def gproj_add_kernel(s, kept, recv, own, o1, o2, o3):
    for j, out in enumerate((own, o1, o2, o3)):
        at = (s[X] + j) % NX
        out[...] = (kept[at] + recv[at].astype(F32)).astype(out.dtype)


def gproj_sum_kernel(s, own, r1, r2, r3, sent, kept):
    z = s[ZH]

    def total(at):
        return own[at] + r1[at].astype(F32) + r2[at].astype(F32) + r3[at].astype(F32)

    sent[...] = total(1 - z).astype(BF)
    kept[...] = total(z)


def sum_over(array, axis, n):
    got = [lax.ppermute(array, axis, ring(n, j)) for j in range(1, n)]
    got = lax.optimization_barrier(got)
    return sum(got, array)


def body(
    queries, keys, values, out_weight, residual, student_hidden, norm_gain, projection, lengths
):
    g, d = lax.axis_index("grp"), lax.axis_index("dp")
    x, zh, c = lax.axis_index("x"), lax.axis_index("zh"), lax.axis_index("core")
    zc = zh * 2 + c
    m = x * 4 + zc
    half = D_T // 2
    blk = D_T // 8
    rows = D_S // 16
    width = D_S // 2
    barrier = lax.optimization_barrier
    scalars = Ordered(
        jnp.concatenate([jnp.stack([x, zc, g, d, zh, c, m * 128]).astype(jnp.int32), lengths])
    )
    swap = ring(2, 1)
    stages = (0, 1)

    def column(stage, near, mine, n):
        def index(i, s):
            return (0, column_block(s, stage, near, mine))

        return pl.BlockSpec((n, blk), index)

    q5 = queries.reshape(NX, 4, 128, 256)
    q_block = (NX, 2, 128, 256)
    along_z, w_out, res_out = call(
        pick_kernel,
        scalars,
        [
            (q5, pl.BlockSpec(q_block, lambda i, s: (0, 1 - s[ZH], 0, 0))),
            *[(out_weight, column(st, near, False, 256)) for near in (False, True) for st in stages],
            *[(residual[0], column(st, True, False, 128)) for st in stages],
        ],
        [(q_block, BF, True), ((256, 4 * blk), BF, True), ((128, 2 * blk), BF, True)],
        "pick",
        pinned=range(7),
    )
    along_z = lax.ppermute(along_z, ("grp", "zh"), WRAP)
    w_other = lax.ppermute(w_out, "core", swap)
    res_other = lax.ppermute(res_out, "core", swap)

    def attend(q, spec, name):
        return call(
            attend_kernel,
            scalars,
            [
                (q, spec),
                (keys[0], pl.BlockSpec((2048, HD), lambda i, s: (0, s[X]))),
                (values[0], pl.BlockSpec((2048, HD), lambda i, s: (0, s[X]))),
            ],
            [((1024, 256), BF)],
            name,
            scratch=[pltpu.VMEM((2048, 2 * HD), BF)],
            mib=40,
        )[0]

    hidden, _ = barrier((student_hidden[0], w_out))
    hidden = hidden.astype(F32)
    inverse_rms = lax.rsqrt(jnp.mean(hidden * hidden, axis=-1, keepdims=True) + 1e-06)
    normed = (hidden * inverse_rms * norm_gain).astype(BF)
    scalars.after(normed)
    normed = lax.all_gather(normed, "dp", axis=0, tiled=True)

    w_z = call(
        pick_weights_kernel,
        scalars,
        [
            *[(out_weight, column(st, False, True, 256)) for st in stages],
            (w_other, pl.BlockSpec((256, 2 * blk), lambda i, s: (0, 0))),
        ],
        [((512, blk), BF, True)] * 2,
        "pick_weights",
        pinned=range(3),
    )
    ctx_a = attend(q5, pl.BlockSpec(q_block, lambda i, s: (0, s[ZH], 0, 0)), "attend_chip")
    w_z = [lax.ppermute(w, ("grp", "zh"), WRAP) for w in w_z]
    ctx_ac = lax.ppermute(ctx_a, "core", swap)
    along_z, _ = barrier((along_z, ctx_a))
    ctx_b = attend(along_z, whole(q_block), "attend_next")
    ctx_bc = lax.ppermute(ctx_b, "core", swap)

    projected = []
    for st in stages:
        own, *outs = call(
            project_kernel,
            scalars,
            [
                *[(ctx, whole((1024, 256))) for ctx in (ctx_a, ctx_ac, ctx_b, ctx_bc)],
                (out_weight, column(st, True, True, 256)),
                (w_other, pl.BlockSpec((256, blk), lambda i, s, st=st: (0, 2 + st))),
                (w_z[st], whole((512, blk))),
            ],
            [((2, 128, blk), F32)] + [((2, 128, blk), BF, True)] * 3,
            f"project_{st}",
            scratch=[pltpu.VMEM((1024, blk), F32)],
        )
        if st == 0:
            normed, _ = barrier((normed, own))
            predicted = jnp.dot(normed, projection, preferred_element_type=F32)
            scalars.after(predicted)
        projected.append((own, {j: lax.ppermute(outs[j - 1], "x", ring(NX, j)) for j in (2, 1, 3)}))

    compared, same, cross = [], [], []
    for st in stages:
        own, got = projected[st]
        done_same, done_cross = call(
            finish_kernel,
            scalars,
            [
                (own, whole((2, 128, blk))),
                *[(got[j], whole((2, 128, blk))) for j in (1, 2, 3)],
                (residual[0], column(st, True, True, 128)),
                (res_other, pl.BlockSpec((128, blk), lambda i, s, st=st: (0, st))),
            ],
            [((128, blk), BF)] * 2,
            f"finish_{st}",
        )
        same.append(done_same)
        cross.append(done_cross)
        compared.append(lax.ppermute(done_same, ("dp", "core"), to_owner(st, False)))
        compared.append(lax.ppermute(done_cross, ("dp", "core"), to_owner(st, True)))

    part = (NX, 2, rows, blk)
    gp, back, small = call(
        compare_kernel,
        scalars,
        [
            (predicted, whole((512, blk))),
            (normed, whole((512, D_S))),
            (projection, whole((D_S, blk))),
            *[(a, whole((128, blk))) for a in compared],
        ],
        [((512, blk), BF, True), ((2, 512, width), BF, True), ((32, 128), F32, True)],
        "compare",
        scratch=[pltpu.VMEM((512, 1), F32)],
    )
    back = back.reshape(1024, width)
    summed = lax.psum_scatter(back, ("grp", "dp"), scatter_dimension=0, tiled=True)

    live_count = jnp.sum(lengths).astype(F32)
    sent, kept = call(
        gproj_kernel,
        scalars,
        [(normed, whole((512, D_S))), (gp, whole((512, blk)))],
        [(part, BF, True), (part, F32)],
        "gproj",
    )
    recv = lax.ppermute(sent, "core", swap)
    own, *outs = call(
        gproj_add_kernel,
        scalars,
        [(kept, whole(part)), (recv, whole(part))],
        [(part[1:], F32)] + [(part[1:], BF, True)] * 3,
        "gproj_add",
    )
    got = {j: lax.ppermute(outs[j - 1], "x", ring(NX, j)) for j in (2, 1, 3)}

    small, _ = barrier((small, own))
    cross = [lax.ppermute(a, "core", swap) for a in barrier((*cross, own))[:2]]
    small = sum_over(small, "dp", 4)
    small = sum_over(small, "grp", 2)
    inner = lax.dynamic_slice_in_dim(small, 21 + d, 1, 0)
    small = sum_over(small, "zh", 2)
    (target,) = call(
        assemble_kernel,
        scalars,
        [(a, whole((128, blk))) for a in (*same, *cross)],
        [((128, half), BF)],
        "assemble",
    )
    scalars.after(small)
    gsent, gkept = call(
        gproj_sum_kernel,
        scalars,
        [(own, whole(part[1:]))] + [(got[j], whole(part[1:])) for j in (1, 2, 3)],
        [((rows, blk), BF, True), ((rows, blk), F32)],
        "gproj_sum",
    )
    gsent = lax.ppermute(gsent, "zh", swap)
    small, _ = barrier((small, gkept))
    small = sum_over(small, "core", 2)
    small = sum_over(small, "x", NX)
    grad_proj = (gkept + gsent.astype(F32)) / live_count
    small = small.reshape(-1)
    distill_loss = small[20 * 128] / (live_count * D_T)
    gain_half = lax.dynamic_slice_in_dim(norm_gain, g * width, width, 0)
    grad_gain = lax.dynamic_slice_in_dim(small, g * width, width, 0) / (gain_half * live_count)

    half_shape = (128, width)
    (grad_hidden,) = call(
        hidden_kernel,
        scalars,
        [
            (summed, whole(half_shape)),
            (inner.reshape(128, 1), whole((128, 1))),
            (student_hidden[0], pl.BlockSpec((128, width), lambda i, s: (0, s[G]))),
            (inverse_rms, whole((128, 1))),
            (norm_gain.reshape(1, D_S), pl.BlockSpec((1, width), lambda i, s: (0, s[G]))),
        ],
        [(half_shape, F32)],
        "hidden",
        pinned=range(1),
    )
    return (target[None], distill_loss, grad_proj, grad_gain, grad_hidden[None])


def solution(mesh):
    fine = Mesh(mesh.devices.reshape(2, 4, 4, 2, 2), ("grp", "dp", "x", "zh", "core"))
    in_specs = (
        P("dp", None, MP),
        P("dp", None, None),
        P("dp", None, None),
        P(MP, None),
        P("dp", MP, None),
        P("dp", MP, None),
        P(),
        P(None, ("grp", "dp")),
        P(),
    )
    out_specs = (P("dp", MP, "grp"), P(), P(MP, ("grp", "dp")), P("grp"), P("dp", MP, "grp"))
    return jax.shard_map(body, mesh=fine, in_specs=in_specs, out_specs=out_specs, check_vma=False)
```

```python
import math

import jax
import jax.numpy as jnp
from jax import lax
from jax.experimental import pallas as pl
from jax.experimental.pallas import tpu as pltpu
from jax.sharding import Mesh
from jax.sharding import PartitionSpec as P

D_T = 5120
D_S = 2560
HD = 128
HQ = 32
KVH = 4

BF = jnp.bfloat16
F32 = jnp.float32
NX = 4
NZ = 4
MP = ("x", "zh", "core")


def ring(n, k):
    return [(i, (i + k) % n) for i in range(n)]


WRAP = [(g * 2 + z, (1 - g) * 2 + (1 - z)) for g in range(2) for z in range(2)]
MIB = 32
COST = 1


def block_of(stage, core):
    return 2 + core if stage == 0 else 1 - core


def to_owner(stage, cross):
    return [
        (d * 2 + c, (d + block_of(stage, c)) % 4 * 2 + (1 - c if cross else c))
        for d in range(4)
        for c in range(2)
    ]


def whole(shape):
    return pl.BlockSpec(shape, lambda i, s: (0,) * len(shape))


def call(kernel, scalars, ins, outs, name, scratch=(), mib=MIB, pinned=(), steps=1, blocked=None):
    outs = pl.pallas_call(
        kernel,
        out_shape=[
            pltpu.HBM(o[0], o[1]) if len(o) == 3 else jax.ShapeDtypeStruct(*o) for o in outs
        ],
        grid_spec=pltpu.PrefetchScalarGridSpec(
            num_scalar_prefetch=1,
            grid=(steps,),
            in_specs=[spec for _, spec in ins],
            out_specs=[(blocked or {}).get(i, whole(o[0])) for i, o in enumerate(outs)],
            scratch_shapes=list(scratch),
        ),
        compiler_params=pltpu.CompilerParams(vmem_limit_bytes=mib * 1024 * 1024),
        cost_estimate=pl.CostEstimate(flops=COST, bytes_accessed=COST, transcendentals=0),
        name=name,
    )(scalars.value, *[
            pltpu.with_memory_space_constraint(a, pltpu.HBM) if i in pinned else a
            for i, (a, _) in enumerate(ins)
        ])
    scalars.after(outs[0])
    return outs


class Ordered:
    def __init__(self, value):
        self.value = value

    def after(self, array):
        self.value, _ = lax.optimization_barrier((self.value, array))


X, ZC, G, D, ZH, C, FIRST, LENGTHS = range(8)


def column_block(s, stage, near, mine):
    core = s[C] if mine else 1 - s[C]
    side = s[G] if near else 1 - s[G]
    return side * 4 + (s[D] + block_of(stage, core)) % 4


def pick_kernel(s, q, w0, w1, w2, w3, res0, res1, q_out, w_out, res_out):
    q_out[...] = q[...]
    for i, w in enumerate((w0, w1, w2, w3)):
        w_out[:, i * 640 : i * 640 + 640] = w[...]
    res_out[:, :640] = res0[...]
    res_out[:, 640:] = res1[...]


def pick_weights_kernel(s, own0, own1, other, out0, out1):
    for i, (own, out) in enumerate(((own0, out0), (own1, out1))):
        out[:256] = own[...]
        out[256:] = other[:, i * 640 : i * 640 + 640]


def attend_kernel(s, q_ref, k_ref, v_ref, out_ref, vext):
    vext[:, :HD] = v_ref[...]
    vext[:, HD:] = jnp.ones((v_ref.shape[0], HD), BF)
    scale = HD ** (-0.5) * math.log2(math.e)
    rows = lax.broadcasted_iota(jnp.int32, (256, 512), 0) % 128
    cols = lax.broadcasted_iota(jnp.int32, (256, 512), 1)
    behind = cols - rows
    for part in range(NX):
        length = 512 * (part + 1)
        for block in range(2):
            q = q_ref[part, block]
            q = jnp.concatenate([q[:, :HD], q[:, HD:]], axis=0)
            scores = lax.dot_general(
                q, k_ref[:length, :], (((1,), (1,)), ((), ())), preferred_element_type=F32
            )
            allowed = behind <= (s[ZH] * 2 + block) * 128
            last = jnp.where(allowed, scores[:, length - 512 :], -1e30)
            if part:
                scores = jnp.concatenate([scores[:, : length - 512], last], axis=1)
            else:
                scores = last
            top = jnp.max(scores, axis=-1, keepdims=True)
            probs = jnp.exp2((scores - top) * scale).astype(BF)
            mixed = jnp.dot(probs, vext[:length, :], preferred_element_type=F32)
            mixed = (mixed[:, :HD] / mixed[:, HD:]).astype(BF)
            at = (block * NX + part) * 128
            out_ref[at : at + 128, :HD] = mixed[:128]
            out_ref[at : at + 128, HD:] = mixed[128:]


def project_kernel(s, ctx_a, ctx_ac, ctx_b, ctx_bc, w_a, w_ac, w_z, own, o1, o2, o3, total):
    def dot(a, b):
        return jnp.dot(a[...], b, preferred_element_type=F32)

    total[...] = (
        dot(ctx_a, w_a[...])
        + dot(ctx_ac, w_ac[...])
        + dot(ctx_b, w_z[:256])
        + dot(ctx_bc, w_z[256:])
    )
    for j, out in enumerate((own, o1, o2, o3)):
        for block in range(2):
            at = pl.multiple_of((block * NX + (s[X] + j) % NX) * 128, 128)
            out[block] = total[pl.ds(at, 128), :].astype(out.dtype)


def finish_kernel(s, own, r1, r2, r3, res, res_other, *refs):
    def rows(at):
        parts = own[at] + r1[at].astype(F32) + r2[at].astype(F32) + r3[at].astype(F32)
        return parts

    same, cross = refs[-2], refs[-1]
    same[...] = (res[...].astype(F32) + rows(s[C])).astype(BF)
    cross[...] = (res_other[...].astype(F32) + rows(1 - s[C])).astype(BF)


def assemble_kernel(s, same0, same1, got0, got1, target):
    for piece, stage, core in (
        (same0, 0, s[C]),
        (same1, 1, s[C]),
        (got0, 0, 1 - s[C]),
        (got1, 1, 1 - s[C]),
    ):
        at = pl.multiple_of(((s[D] + block_of(stage, core)) % 4) * 640, 128)
        target[:, pl.ds(at, 640)] = piece[...]


def compare_kernel(s, pred, normed, proj, sm0, cr0, sm1, cr1, gp, back, small, inner):
    step = pl.program_id(0)

    @pl.when(step == 0)
    def _():
        differences(s, pred, (sm0, cr0, sm1, cr1), gp, small, inner)

    for part in range(2):
        base = pl.multiple_of((step * 2 + part) * 640, 128)
        grad = lax.dot_general(
            gp[...], proj[pl.ds(base, 640), :], (((1,), (1,)), ((), ())), preferred_element_type=F32
        )
        back[0, :, part * 640 : part * 640 + 640] = grad.astype(BF)
        gain = jnp.sum(grad * normed[:, pl.ds(base, 640)].astype(F32), axis=0, keepdims=True)
        for i in range(5):
            small[pl.ds((step * 2 + part) * 5 + i, 1), :] = gain[:, i * 128 : i * 128 + 128]


def differences(s, pred, gots, gp, small, inner):
    sm0, cr0, sm1, cr1 = gots
    square = jnp.zeros((1, 640), F32)
    for got, stage, core in (
        (sm0, 0, s[C]),
        (cr0, 0, 1 - s[C]),
        (sm1, 1, s[C]),
        (cr1, 1, 1 - s[C]),
    ):
        seq = (s[D] + 4 - block_of(stage, core)) % 4
        at = pl.multiple_of(seq * 128, 128)
        live = lax.broadcasted_iota(jnp.int32, (128, 640), 0) < s[LENGTHS + seq] - s[FIRST]
        here = pred[pl.ds(at, 128), :]
        diff = jnp.where(live, here - got[...].astype(F32), 0.0)
        square = square + jnp.sum(diff * diff, axis=0, keepdims=True)
        rounded = diff.astype(BF)
        gp[pl.ds(at, 128), :] = rounded
        inner[pl.ds(at, 128), :] = jnp.sum(rounded.astype(F32) * here, axis=-1, keepdims=True)
    small[...] = jnp.zeros((32, 128), F32)
    small[20:21, :] = jnp.broadcast_to(jnp.sum(square, axis=-1, keepdims=True), (1, 128))
    turned = jnp.broadcast_to(inner[...], (512, 128)).T
    for i in range(4):
        small[21 + i : 22 + i, :] = turned[:1, i * 128 : i * 128 + 128]


def hidden_kernel(s, grad, inner, hidden, inverse_rms, norm_gain, out):
    scale = inverse_rms[...]
    unit = hidden[...].astype(F32) * scale
    out[...] = scale * (grad[...].astype(F32) * norm_gain[...] - unit * (inner[...] / D_S))


def gproj_kernel(s, normed, gp, sent, kept):
    first = s[C] == 0
    for part in range(NX):
        total = lax.dot_general(
            normed[:, part * 640 : part * 640 + 640],
            gp[...],
            (((0,), (0,)), ((), ())),
            preferred_element_type=F32,
        )
        for z in range(2):
            low = total[z * 320 : z * 320 + 160]
            high = total[z * 320 + 160 : z * 320 + 320]
            sent[part, z] = jnp.where(first, high, low).astype(BF)
            kept[part, z] = jnp.where(first, low, high)


def gproj_add_kernel(s, kept, recv, own, o1, o2, o3):
    for j, out in enumerate((own, o1, o2, o3)):
        at = (s[X] + j) % NX
        out[...] = (kept[at] + recv[at].astype(F32)).astype(out.dtype)


def gproj_sum_kernel(s, own, r1, r2, r3, sent, kept):
    z = s[ZH]

    def total(at):
        return own[at] + r1[at].astype(F32) + r2[at].astype(F32) + r3[at].astype(F32)

    sent[...] = total(1 - z).astype(BF)
    kept[...] = total(z)


def sum_over(array, axis, n):
    got = [lax.ppermute(array, axis, ring(n, j)) for j in range(1, n)]
    got = lax.optimization_barrier(got)
    return sum(got, array)


def body(
    queries, keys, values, out_weight, residual, student_hidden, norm_gain, projection, lengths
):
    g, d = lax.axis_index("grp"), lax.axis_index("dp")
    x, zh, c = lax.axis_index("x"), lax.axis_index("zh"), lax.axis_index("core")
    zc = zh * 2 + c
    m = x * 4 + zc
    half = D_T // 2
    blk = D_T // 8
    rows = D_S // 16
    width = D_S // 2
    barrier = lax.optimization_barrier
    scalars = Ordered(
        jnp.concatenate([jnp.stack([x, zc, g, d, zh, c, m * 128]).astype(jnp.int32), lengths])
    )
    swap = ring(2, 1)
    stages = (0, 1)

    def column(stage, near, mine, n):
        def index(i, s):
            return (0, column_block(s, stage, near, mine))

        return pl.BlockSpec((n, blk), index)

    q5 = queries.reshape(NX, 4, 128, 256)
    q_block = (NX, 2, 128, 256)
    along_z, w_out, res_out = call(
        pick_kernel,
        scalars,
        [
            (q5, pl.BlockSpec(q_block, lambda i, s: (0, 1 - s[ZH], 0, 0))),
            *[(out_weight, column(st, near, False, 256)) for near in (False, True) for st in stages],
            *[(residual[0], column(st, True, False, 128)) for st in stages],
        ],
        [(q_block, BF, True), ((256, 4 * blk), BF, True), ((128, 2 * blk), BF, True)],
        "pick",
        pinned=range(7),
    )
    along_z = lax.ppermute(along_z, ("grp", "zh"), WRAP)
    w_other = lax.ppermute(w_out, "core", swap)
    res_other = lax.ppermute(res_out, "core", swap)

    def attend(q, spec, name):
        return call(
            attend_kernel,
            scalars,
            [
                (q, spec),
                (keys[0], pl.BlockSpec((2048, HD), lambda i, s: (0, s[X]))),
                (values[0], pl.BlockSpec((2048, HD), lambda i, s: (0, s[X]))),
            ],
            [((1024, 256), BF)],
            name,
            scratch=[pltpu.VMEM((2048, 2 * HD), BF)],
            mib=40,
        )[0]

    hidden, _ = barrier((student_hidden[0], w_out))
    hidden = hidden.astype(F32)
    inverse_rms = lax.rsqrt(jnp.mean(hidden * hidden, axis=-1, keepdims=True) + 1e-06)
    normed = (hidden * inverse_rms * norm_gain).astype(BF)
    scalars.after(normed)
    normed = lax.all_gather(normed, "dp", axis=0, tiled=True)

    w_z = call(
        pick_weights_kernel,
        scalars,
        [
            *[(out_weight, column(st, False, True, 256)) for st in stages],
            (w_other, pl.BlockSpec((256, 2 * blk), lambda i, s: (0, 0))),
        ],
        [((512, blk), BF, True)] * 2,
        "pick_weights",
        pinned=range(3),
    )
    ctx_a = attend(q5, pl.BlockSpec(q_block, lambda i, s: (0, s[ZH], 0, 0)), "attend_chip")
    w_z = [lax.ppermute(w, ("grp", "zh"), WRAP) for w in w_z]
    ctx_ac = lax.ppermute(ctx_a, "core", swap)
    along_z, _ = barrier((along_z, ctx_a))
    ctx_b = attend(along_z, whole(q_block), "attend_next")
    ctx_bc = lax.ppermute(ctx_b, "core", swap)

    projected = []
    for st in stages:
        own, *outs = call(
            project_kernel,
            scalars,
            [
                *[(ctx, whole((1024, 256))) for ctx in (ctx_a, ctx_ac, ctx_b, ctx_bc)],
                (out_weight, column(st, True, True, 256)),
                (w_other, pl.BlockSpec((256, blk), lambda i, s, st=st: (0, 2 + st))),
                (w_z[st], whole((512, blk))),
            ],
            [((2, 128, blk), F32)] + [((2, 128, blk), BF, True)] * 3,
            f"project_{st}",
            scratch=[pltpu.VMEM((1024, blk), F32)],
        )
        if st == 0:
            normed, _ = barrier((normed, own))
            predicted = jnp.dot(normed, projection, preferred_element_type=F32)
            scalars.after(predicted)
        projected.append((own, {j: lax.ppermute(outs[j - 1], "x", ring(NX, j)) for j in (2, 1, 3)}))

    compared, same, cross = [], [], []
    for st in stages:
        own, got = projected[st]
        done_same, done_cross = call(
            finish_kernel,
            scalars,
            [
                (own, whole((2, 128, blk))),
                *[(got[j], whole((2, 128, blk))) for j in (1, 2, 3)],
                (residual[0], column(st, True, True, 128)),
                (res_other, pl.BlockSpec((128, blk), lambda i, s, st=st: (0, st))),
            ],
            [((128, blk), BF)] * 2,
            f"finish_{st}",
        )
        same.append(done_same)
        cross.append(done_cross)
        compared.append(lax.ppermute(done_same, ("dp", "core"), to_owner(st, False)))
        compared.append(lax.ppermute(done_cross, ("dp", "core"), to_owner(st, True)))

    part = (NX, 2, rows, blk)
    gp, back, small = call(
        compare_kernel,
        scalars,
        [
            (predicted, whole((512, blk))),
            (normed, whole((512, D_S))),
            (projection, whole((D_S, blk))),
            *[(a, whole((128, blk))) for a in compared],
        ],
        [((512, blk), BF, True), ((2, 512, width), BF, True), ((32, 128), F32, True)],
        "compare",
        scratch=[pltpu.VMEM((512, 1), F32)],
        steps=2,
        blocked={1: pl.BlockSpec((1, 512, width), lambda i, s: (i, 0, 0))},
    )
    back = back.reshape(1024, width)
    summed = lax.psum_scatter(back, ("grp", "dp"), scatter_dimension=0, tiled=True)

    live_count = jnp.sum(lengths).astype(F32)
    sent, kept = call(
        gproj_kernel,
        scalars,
        [(normed, whole((512, D_S))), (gp, whole((512, blk)))],
        [(part, BF, True), (part, F32)],
        "gproj",
    )
    recv = lax.ppermute(sent, "core", swap)
    inner = small[21:25]
    small = sum_over(small[:21], "x", NX)
    small, _ = barrier((jnp.concatenate([small, inner]), sent))
    recv, small = barrier((recv, small))
    own, *outs = call(
        gproj_add_kernel,
        scalars,
        [(kept, whole(part)), (recv, whole(part))],
        [(part[1:], F32)] + [(part[1:], BF, True)] * 3,
        "gproj_add",
    )
    got = {j: lax.ppermute(outs[j - 1], "x", ring(NX, j)) for j in (2, 1, 3)}

    cross = [lax.ppermute(a, "core", swap) for a in barrier((*cross, own))[:2]]
    small, _ = barrier((small, own))
    small = sum_over(small, "dp", 4)
    small = sum_over(small, "grp", 2)
    inner = lax.dynamic_slice_in_dim(small, 21 + d, 1, 0)
    small = sum_over(small[:21], "zh", 2)
    (target,) = call(
        assemble_kernel,
        scalars,
        [(a, whole((128, blk))) for a in (*same, *cross)],
        [((128, half), BF)],
        "assemble",
    )
    scalars.after(small)
    gsent, gkept = call(
        gproj_sum_kernel,
        scalars,
        [(own, whole(part[1:]))] + [(got[j], whole(part[1:])) for j in (1, 2, 3)],
        [((rows, blk), BF, True), ((rows, blk), F32)],
        "gproj_sum",
    )
    gsent = lax.ppermute(gsent, "zh", swap)
    small, _ = barrier((small, gkept))
    small = sum_over(small, "core", 2)
    small = small.reshape(-1)
    distill_loss = small[20 * 128] / (live_count * D_T)
    gain_half = lax.dynamic_slice_in_dim(norm_gain, g * width, width, 0)
    grad_gain = lax.dynamic_slice_in_dim(small, g * width, width, 0) / (gain_half * live_count)

    half_shape = (128, width)
    (grad_hidden,) = call(
        hidden_kernel,
        scalars,
        [
            (summed, whole(half_shape)),
            (inner.reshape(128, 1), whole((128, 1))),
            (student_hidden[0], pl.BlockSpec((128, width), lambda i, s: (0, s[G]))),
            (inverse_rms, whole((128, 1))),
            (norm_gain.reshape(1, D_S), pl.BlockSpec((1, width), lambda i, s: (0, s[G]))),
        ],
        [(half_shape, F32)],
        "hidden",
        pinned=range(1),
    )
    gsent, grad_hidden = barrier((gsent, grad_hidden))
    grad_proj = (gkept + gsent.astype(F32)) / live_count
    return (target[None], distill_loss, grad_proj, grad_gain, grad_hidden[None])


def solution(mesh):
    fine = Mesh(mesh.devices.reshape(2, 4, 4, 2, 2), ("grp", "dp", "x", "zh", "core"))
    in_specs = (
        P("dp", None, MP),
        P("dp", None, None),
        P("dp", None, None),
        P(MP, None),
        P("dp", MP, None),
        P("dp", MP, None),
        P(),
        P(None, ("grp", "dp")),
        P(),
    )
    out_specs = (P("dp", MP, "grp"), P(), P(MP, ("grp", "dp")), P("grp"), P("dp", MP, "grp"))
    return jax.shard_map(body, mesh=fine, in_specs=in_specs, out_specs=out_specs, check_vma=False)
```

```python
import functools
import math

import jax
import jax.numpy as jnp
from jax import lax
from jax.experimental import pallas as pl
from jax.experimental.pallas import tpu as pltpu
from jax.sharding import Mesh
from jax.sharding import PartitionSpec as P

D_T = 5120
D_S = 2560
HD = 128
HQ = 32
KVH = 4

BF = jnp.bfloat16
F32 = jnp.float32
NX = 4
NZ = 4
MP = ("x", "zh", "core")


def ring(n, k):
    return [(i, (i + k) % n) for i in range(n)]


WRAP = [(g * 2 + z, (1 - g) * 2 + (1 - z)) for g in range(2) for z in range(2)]
MIB = 32
COST = 1
IN_HBM = pl.BlockSpec(memory_space=pltpu.HBM)


def block_of(stage, core):
    return 2 + core if stage == 0 else 1 - core


def to_owner(stage, cross):
    return [
        (d * 2 + c, (d + block_of(stage, c)) % 4 * 2 + (1 - c if cross else c))
        for d in range(4)
        for c in range(2)
    ]


def whole(shape):
    return pl.BlockSpec(shape, lambda i, s: (0,) * len(shape))


def call(kernel, scalars, ins, outs, name, scratch=(), mib=MIB, pinned=(), steps=1, blocked=None, aliases=None):
    outs = pl.pallas_call(
        kernel,
        out_shape=[
            pltpu.HBM(o[0], o[1]) if len(o) == 3 else jax.ShapeDtypeStruct(*o) for o in outs
        ],
        grid_spec=pltpu.PrefetchScalarGridSpec(
            num_scalar_prefetch=1,
            grid=(steps,),
            in_specs=[spec for _, spec in ins],
            out_specs=[(blocked or {}).get(i, whole(o[0])) for i, o in enumerate(outs)],
            scratch_shapes=list(scratch),
        ),
        compiler_params=pltpu.CompilerParams(vmem_limit_bytes=mib * 1024 * 1024),
        cost_estimate=pl.CostEstimate(flops=COST, bytes_accessed=COST, transcendentals=0),
        input_output_aliases=aliases or {},
        name=name,
    )(scalars.value, *[
            pltpu.with_memory_space_constraint(a, pltpu.HBM) if i in pinned else a
            for i, (a, _) in enumerate(ins)
        ])
    scalars.after(outs[0])
    return outs


class Ordered:
    def __init__(self, value):
        self.value = value

    def after(self, array):
        self.value, _ = lax.optimization_barrier((self.value, array))


X, ZC, G, D, ZH, C, FIRST, LENGTHS = range(8)


def column_block(s, stage, near, mine):
    core = s[C] if mine else 1 - s[C]
    side = s[G] if near else 1 - s[G]
    return side * 4 + (s[D] + block_of(stage, core)) % 4


def pick_kernel(s, q, w0, w1, w2, w3, res0, res1, q_out, w_out, res_out):
    q_out[...] = q[...]
    for i, w in enumerate((w0, w1, w2, w3)):
        w_out[:, i * 640 : i * 640 + 640] = w[...]
    res_out[:, :640] = res0[...]
    res_out[:, 640:] = res1[...]


def pick_weights_kernel(s, own0, own1, other, out0, out1):
    for i, (own, out) in enumerate(((own0, out0), (own1, out1))):
        out[:256] = own[...]
        out[256:] = other[:, i * 640 : i * 640 + 640]


def attend_kernel(s, q_ref, k_ref, v_ref, out_ref, vext):
    vext[:, :HD] = v_ref[...]
    vext[:, HD:] = jnp.ones((v_ref.shape[0], HD), BF)
    scale = HD ** (-0.5) * math.log2(math.e)
    rows = lax.broadcasted_iota(jnp.int32, (256, 512), 0) % 128
    cols = lax.broadcasted_iota(jnp.int32, (256, 512), 1)
    behind = cols - rows
    for part in range(NX):
        length = 512 * (part + 1)
        for block in range(2):
            q = q_ref[part, block]
            q = jnp.concatenate([q[:, :HD], q[:, HD:]], axis=0)
            scores = lax.dot_general(
                q, k_ref[:length, :], (((1,), (1,)), ((), ())), preferred_element_type=F32
            )
            allowed = behind <= (s[ZH] * 2 + block) * 128
            last = jnp.where(allowed, scores[:, length - 512 :], -1e30)
            if part:
                scores = jnp.concatenate([scores[:, : length - 512], last], axis=1)
            else:
                scores = last
            top = jnp.max(scores, axis=-1, keepdims=True)
            probs = jnp.exp2((scores - top) * scale).astype(BF)
            mixed = jnp.dot(probs, vext[:length, :], preferred_element_type=F32)
            mixed = (mixed[:, :HD] / mixed[:, HD:]).astype(BF)
            at = (block * NX + part) * 128
            out_ref[at : at + 128, :HD] = mixed[:128]
            out_ref[at : at + 128, HD:] = mixed[128:]


def project_kernel(s, ctx_a, ctx_ac, ctx_b, ctx_bc, w_a, w_ac, w_z, own, o1, o2, o3, total):
    def dot(a, b):
        return jnp.dot(a[...], b, preferred_element_type=F32)

    total[...] = (
        dot(ctx_a, w_a[...])
        + dot(ctx_ac, w_ac[...])
        + dot(ctx_b, w_z[:256])
        + dot(ctx_bc, w_z[256:])
    )
    for j, out in enumerate((own, o1, o2, o3)):
        for block in range(2):
            at = pl.multiple_of((block * NX + (s[X] + j) % NX) * 128, 128)
            out[block] = total[pl.ds(at, 128), :].astype(out.dtype)


def finish_kernel(s, own, r1, r2, r3, res, res_other, *refs):
    def rows(at):
        parts = own[at] + r1[at].astype(F32) + r2[at].astype(F32) + r3[at].astype(F32)
        return parts

    same, cross = refs[-2], refs[-1]
    same[...] = (res[...].astype(F32) + rows(s[C])).astype(BF)
    cross[...] = (res_other[...].astype(F32) + rows(1 - s[C])).astype(BF)


def assemble_kernel(s, same0, same1, got0, got1, target):
    for piece, stage, core in (
        (same0, 0, s[C]),
        (same1, 1, s[C]),
        (got0, 0, 1 - s[C]),
        (got1, 1, 1 - s[C]),
    ):
        at = pl.multiple_of(((s[D] + block_of(stage, core)) % 4) * 640, 128)
        target[:, pl.ds(at, 640)] = piece[...]


def compare_kernel(stage, s, pred, normed, proj, got_same, got_cross, *refs):
    before, (gp_out, back_out, small, gp, back, sems) = refs[:-6], refs[-6:]
    if stage == 0:
        small[...] = jnp.zeros((32, 128), F32)
    else:
        small[...] = before[2][...]
    square = jnp.zeros((1, 640), F32)
    inner, starts, copies = [], [], []
    for i, (got, core) in enumerate(((got_same, s[C]), (got_cross, 1 - s[C]))):
        seq = (s[D] + 4 - block_of(stage, core)) % 4
        at = pl.multiple_of(seq * 128, 128)
        starts.append((seq, at))
        live = lax.broadcasted_iota(jnp.int32, (128, 640), 0) < s[LENGTHS + seq] - s[FIRST]
        here = pred[pl.ds(at, 128), :]
        diff = jnp.where(live, here - got[...].astype(F32), 0.0)
        square = square + jnp.sum(diff * diff, axis=0, keepdims=True)
        rounded = diff.astype(BF)
        gp[i * 128 : i * 128 + 128] = rounded
        inner.append(jnp.sum(rounded.astype(F32) * here, axis=-1, keepdims=True))
        copies.append(
            pltpu.make_async_copy(gp.at[pl.ds(i * 128, 128)], gp_out.at[pl.ds(at, 128)], sems.at[i])
        )
        copies[-1].start()
    small[20:21, :] = small[20:21, :] + jnp.sum(square, axis=-1, keepdims=True)
    turned = jnp.broadcast_to(jnp.concatenate(inner, axis=0), (256, 128)).T
    for i, (seq, _) in enumerate(starts):
        small[pl.ds(21 + seq, 1), :] = turned[:1, i * 128 : i * 128 + 128]
    for half in range(2):
        for part in range(2):
            base = half * 1280 + part * 640
            grad = lax.dot_general(
                gp[...], proj[base : base + 640, :], (((1,), (1,)), ((), ())), preferred_element_type=F32
            )
            total = jnp.zeros((128, 640), F32)
            for i, (_, at) in enumerate(starts):
                rows = grad[i * 128 : i * 128 + 128]
                back[half, i, :, part * 640 : part * 640 + 640] = rows.astype(BF)
                total = total + rows * normed[pl.ds(at, 128), base : base + 640].astype(F32)
            gain = jnp.sum(total, axis=0, keepdims=True)
            for i in range(5):
                row = base // 128 + i
                small[row : row + 1, :] = small[row : row + 1, :] + gain[:, i * 128 : i * 128 + 128]
        for i, (_, at) in enumerate(starts):
            copies.append(
                pltpu.make_async_copy(
                    back.at[half, i], back_out.at[half, pl.ds(at, 128)], sems.at[2 + half * 2 + i]
                )
            )
            copies[-1].start()
    for copy in copies:
        copy.wait()


def hidden_kernel(s, grad, inner, hidden, inverse_rms, norm_gain, out):
    scale = inverse_rms[...]
    unit = hidden[...].astype(F32) * scale
    out[...] = scale * (grad[...].astype(F32) * norm_gain[...] - unit * (inner[...] / D_S))


def gproj_kernel(s, normed, gp, sent, kept):
    first = s[C] == 0
    for part in range(NX):
        total = lax.dot_general(
            normed[:, part * 640 : part * 640 + 640],
            gp[...],
            (((0,), (0,)), ((), ())),
            preferred_element_type=F32,
        )
        for z in range(2):
            low = total[z * 320 : z * 320 + 160]
            high = total[z * 320 + 160 : z * 320 + 320]
            sent[part, z] = jnp.where(first, high, low).astype(BF)
            kept[part, z] = jnp.where(first, low, high)


def gproj_add_kernel(s, kept, recv, own, o1, o2, o3):
    for j, out in enumerate((own, o1, o2, o3)):
        at = (s[X] + j) % NX
        out[...] = (kept[at] + recv[at].astype(F32)).astype(out.dtype)


def gproj_sum_kernel(s, own, r1, r2, r3, sent, kept):
    z = s[ZH]

    def total(at):
        return own[at] + r1[at].astype(F32) + r2[at].astype(F32) + r3[at].astype(F32)

    sent[...] = total(1 - z).astype(BF)
    kept[...] = total(z)


def sum_over(array, axis, n):
    got = [lax.ppermute(array, axis, ring(n, j)) for j in range(1, n)]
    got = lax.optimization_barrier(got)
    return sum(got, array)


def body(
    queries, keys, values, out_weight, residual, student_hidden, norm_gain, projection, lengths
):
    g, d = lax.axis_index("grp"), lax.axis_index("dp")
    x, zh, c = lax.axis_index("x"), lax.axis_index("zh"), lax.axis_index("core")
    zc = zh * 2 + c
    m = x * 4 + zc
    half = D_T // 2
    blk = D_T // 8
    rows = D_S // 16
    width = D_S // 2
    barrier = lax.optimization_barrier
    scalars = Ordered(
        jnp.concatenate([jnp.stack([x, zc, g, d, zh, c, m * 128]).astype(jnp.int32), lengths])
    )
    swap = ring(2, 1)
    stages = (0, 1)

    def column(stage, near, mine, n):
        def index(i, s):
            return (0, column_block(s, stage, near, mine))

        return pl.BlockSpec((n, blk), index)

    q5 = queries.reshape(NX, 4, 128, 256)
    q_block = (NX, 2, 128, 256)
    along_z, w_out, res_out = call(
        pick_kernel,
        scalars,
        [
            (q5, pl.BlockSpec(q_block, lambda i, s: (0, 1 - s[ZH], 0, 0))),
            *[(out_weight, column(st, near, False, 256)) for near in (False, True) for st in stages],
            *[(residual[0], column(st, True, False, 128)) for st in stages],
        ],
        [(q_block, BF, True), ((256, 4 * blk), BF, True), ((128, 2 * blk), BF, True)],
        "pick",
        pinned=range(7),
    )
    along_z = lax.ppermute(along_z, ("grp", "zh"), WRAP)
    w_other = lax.ppermute(w_out, "core", swap)
    res_other = lax.ppermute(res_out, "core", swap)

    def attend(q, spec, name):
        return call(
            attend_kernel,
            scalars,
            [
                (q, spec),
                (keys[0], pl.BlockSpec((2048, HD), lambda i, s: (0, s[X]))),
                (values[0], pl.BlockSpec((2048, HD), lambda i, s: (0, s[X]))),
            ],
            [((1024, 256), BF)],
            name,
            scratch=[pltpu.VMEM((2048, 2 * HD), BF)],
            mib=40,
        )[0]

    hidden, _ = barrier((student_hidden[0], w_out))
    hidden = hidden.astype(F32)
    inverse_rms = lax.rsqrt(jnp.mean(hidden * hidden, axis=-1, keepdims=True) + 1e-06)
    normed = (hidden * inverse_rms * norm_gain).astype(BF)
    scalars.after(normed)
    normed = lax.all_gather(normed, "dp", axis=0, tiled=True)

    w_z = call(
        pick_weights_kernel,
        scalars,
        [
            *[(out_weight, column(st, False, True, 256)) for st in stages],
            (w_other, pl.BlockSpec((256, 2 * blk), lambda i, s: (0, 0))),
        ],
        [((512, blk), BF, True)] * 2,
        "pick_weights",
        pinned=range(3),
    )
    ctx_a = attend(q5, pl.BlockSpec(q_block, lambda i, s: (0, s[ZH], 0, 0)), "attend_chip")
    w_z = [lax.ppermute(w, ("grp", "zh"), WRAP) for w in w_z]
    ctx_ac = lax.ppermute(ctx_a, "core", swap)
    along_z, _ = barrier((along_z, ctx_a))
    ctx_b = attend(along_z, whole(q_block), "attend_next")
    ctx_bc = lax.ppermute(ctx_b, "core", swap)

    projected = []
    for st in stages:
        own, *outs = call(
            project_kernel,
            scalars,
            [
                *[(ctx, whole((1024, 256))) for ctx in (ctx_a, ctx_ac, ctx_b, ctx_bc)],
                (out_weight, column(st, True, True, 256)),
                (w_other, pl.BlockSpec((256, blk), lambda i, s, st=st: (0, 2 + st))),
                (w_z[st], whole((512, blk))),
            ],
            [((2, 128, blk), F32)] + [((2, 128, blk), BF, True)] * 3,
            f"project_{st}",
            scratch=[pltpu.VMEM((1024, blk), F32)],
        )
        if st == 0:
            normed, _ = barrier((normed, own))
            predicted = jnp.dot(normed, projection, preferred_element_type=F32)
            scalars.after(predicted)
        projected.append((own, {j: lax.ppermute(outs[j - 1], "x", ring(NX, j)) for j in (2, 1, 3)}))

    same, cross, arrived, written = [], [], [], ()
    for st in stages:
        own, got = projected[st]
        done_same, done_cross = call(
            finish_kernel,
            scalars,
            [
                (own, whole((2, 128, blk))),
                *[(got[j], whole((2, 128, blk))) for j in (1, 2, 3)],
                (residual[0], column(st, True, True, 128)),
                (res_other, pl.BlockSpec((128, blk), lambda i, s, st=st: (0, st))),
            ],
            [((128, blk), BF)] * 2,
            f"finish_{st}",
        )
        same.append(done_same)
        cross.append(done_cross)
        arrived.append(
            (
                lax.ppermute(done_same, ("dp", "core"), to_owner(st, False)),
                lax.ppermute(done_cross, ("dp", "core"), to_owner(st, True)),
            )
        )
    for st in stages:
        specs = (IN_HBM, IN_HBM, whole((32, 128)))
        written = call(
            functools.partial(compare_kernel, st),
            scalars,
            [
                (predicted, whole((512, blk))),
                (normed, whole((512, D_S))),
                (projection, whole((D_S, blk))),
                *[(a, whole((128, blk))) for a in arrived[st]],
                *zip(written, specs),
            ],
            [((512, blk), BF, True), ((2, 512, width), BF, True), ((32, 128), F32)],
            f"compare_{st}",
            scratch=[
                pltpu.VMEM((256, blk), BF),
                pltpu.VMEM((2, 2, 128, width), BF),
                pltpu.SemaphoreType.DMA((6,)),
            ],
            pinned=(5, 6) if st else (),
            blocked={0: IN_HBM, 1: IN_HBM},
            aliases={6: 0, 7: 1} if st else {},
        )
    gp, back, small = written
    part = (NX, 2, rows, blk)
    back = back.reshape(1024, width)
    summed = lax.psum_scatter(back, ("grp", "dp"), scatter_dimension=0, tiled=True)

    live_count = jnp.sum(lengths).astype(F32)
    sent, kept = call(
        gproj_kernel,
        scalars,
        [(normed, whole((512, D_S))), (gp, whole((512, blk)))],
        [(part, BF, True), (part, F32)],
        "gproj",
    )
    recv = lax.ppermute(sent, "core", swap)
    inner = small[21:25]
    small = sum_over(small[:21], "x", NX)
    small, _ = barrier((jnp.concatenate([small, inner]), sent))
    own, *outs = call(
        gproj_add_kernel,
        scalars,
        [(kept, whole(part)), (recv, whole(part))],
        [(part[1:], F32)] + [(part[1:], BF, True)] * 3,
        "gproj_add",
    )
    got = {j: lax.ppermute(outs[j - 1], "x", ring(NX, j)) for j in (2, 1, 3)}

    cross = [lax.ppermute(a, "core", swap) for a in barrier((*cross, own))[:2]]
    small, _ = barrier((small, own))
    small = sum_over(small, "dp", 4)
    along = barrier([lax.ppermute(small, ("grp", "zh"), ring(NZ, j)) for j in (1, 2, 3)])
    inner = lax.dynamic_slice_in_dim(small + along[1], 21 + d, 1, 0)
    small = sum(along, small)[:21]
    (target,) = call(
        assemble_kernel,
        scalars,
        [(a, whole((128, blk))) for a in (*same, *cross)],
        [((128, half), BF)],
        "assemble",
    )
    scalars.after(small)
    gsent, gkept = call(
        gproj_sum_kernel,
        scalars,
        [(own, whole(part[1:]))] + [(got[j], whole(part[1:])) for j in (1, 2, 3)],
        [((rows, blk), BF, True), ((rows, blk), F32)],
        "gproj_sum",
    )
    gsent = lax.ppermute(gsent, "zh", swap)
    small, _ = barrier((small, gkept))
    small = sum_over(small, "core", 2)
    small = small.reshape(-1)
    distill_loss = small[20 * 128] / (live_count * D_T)
    gain_half = lax.dynamic_slice_in_dim(norm_gain, g * width, width, 0)
    grad_gain = lax.dynamic_slice_in_dim(small, g * width, width, 0) / (gain_half * live_count)

    half_shape = (128, width)
    (grad_hidden,) = call(
        hidden_kernel,
        scalars,
        [
            (summed, whole(half_shape)),
            (inner.reshape(128, 1), whole((128, 1))),
            (student_hidden[0], pl.BlockSpec((128, width), lambda i, s: (0, s[G]))),
            (inverse_rms, whole((128, 1))),
            (norm_gain.reshape(1, D_S), pl.BlockSpec((1, width), lambda i, s: (0, s[G]))),
        ],
        [(half_shape, F32)],
        "hidden",
        pinned=range(1),
    )
    gsent, grad_hidden = barrier((gsent, grad_hidden))
    grad_proj = (gkept + gsent.astype(F32)) / live_count
    return (target[None], distill_loss, grad_proj, grad_gain, grad_hidden[None])


def solution(mesh):
    fine = Mesh(mesh.devices.reshape(2, 4, 4, 2, 2), ("grp", "dp", "x", "zh", "core"))
    in_specs = (
        P("dp", None, MP),
        P("dp", None, None),
        P("dp", None, None),
        P(MP, None),
        P("dp", MP, None),
        P("dp", MP, None),
        P(),
        P(None, ("grp", "dp")),
        P(),
    )
    out_specs = (P("dp", MP, "grp"), P(), P(MP, ("grp", "dp")), P("grp"), P("dp", MP, "grp"))
    return jax.shard_map(body, mesh=fine, in_specs=in_specs, out_specs=out_specs, check_vma=False)
```

```python
import functools
import math

import jax
import jax.numpy as jnp
from jax import lax
from jax.experimental import pallas as pl
from jax.experimental.pallas import tpu as pltpu
from jax.sharding import Mesh
from jax.sharding import PartitionSpec as P

D_T = 5120
D_S = 2560
HD = 128
HQ = 32
KVH = 4

BF = jnp.bfloat16
F32 = jnp.float32
NX = 4
NZ = 4
MP = ("x", "zh", "core")


def ring(n, k):
    return [(i, (i + k) % n) for i in range(n)]


WRAP = [(g * 2 + z, (1 - g) * 2 + (1 - z)) for g in range(2) for z in range(2)]
MIB = 32
COST = 1
IN_HBM = pl.BlockSpec(memory_space=pltpu.HBM)


def block_of(stage, core):
    return 2 + core if stage == 0 else 1 - core


def to_owner(stage, cross):
    return [
        (d * 2 + c, (d + block_of(stage, c)) % 4 * 2 + (1 - c if cross else c))
        for d in range(4)
        for c in range(2)
    ]


def whole(shape):
    return pl.BlockSpec(shape, lambda i, s: (0,) * len(shape))


def call(kernel, scalars, ins, outs, name, scratch=(), mib=MIB, pinned=(), steps=1, blocked=None, aliases=None):
    outs = pl.pallas_call(
        kernel,
        out_shape=[
            pltpu.HBM(o[0], o[1]) if len(o) == 3 else jax.ShapeDtypeStruct(*o) for o in outs
        ],
        grid_spec=pltpu.PrefetchScalarGridSpec(
            num_scalar_prefetch=1,
            grid=(steps,),
            in_specs=[spec for _, spec in ins],
            out_specs=[(blocked or {}).get(i, whole(o[0])) for i, o in enumerate(outs)],
            scratch_shapes=list(scratch),
        ),
        compiler_params=pltpu.CompilerParams(vmem_limit_bytes=mib * 1024 * 1024),
        cost_estimate=pl.CostEstimate(flops=COST, bytes_accessed=COST, transcendentals=0),
        input_output_aliases=aliases or {},
        name=name,
    )(scalars.value, *[
            pltpu.with_memory_space_constraint(a, pltpu.HBM) if i in pinned else a
            for i, (a, _) in enumerate(ins)
        ])
    scalars.after(outs[0])
    return outs


class Ordered:
    def __init__(self, value):
        self.value = value

    def after(self, array):
        self.value, _ = lax.optimization_barrier((self.value, array))


X, ZC, G, D, ZH, C, FIRST, LENGTHS = range(8)


def column_block(s, stage, near, mine):
    core = s[C] if mine else 1 - s[C]
    side = s[G] if near else 1 - s[G]
    return side * 4 + (s[D] + block_of(stage, core)) % 4


def pick_kernel(s, q, w0, w1, w2, w3, res0, res1, q_out, w_out, res_out):
    q_out[...] = q[...]
    for i, w in enumerate((w0, w1, w2, w3)):
        w_out[:, i * 640 : i * 640 + 640] = w[...]
    res_out[:, :640] = res0[...]
    res_out[:, 640:] = res1[...]


def pick_weights_kernel(s, own0, own1, other, out0, out1):
    for i, (own, out) in enumerate(((own0, out0), (own1, out1))):
        out[:256] = own[...]
        out[256:] = other[:, i * 640 : i * 640 + 640]


def attend_kernel(s, q_ref, k_ref, v_ref, out_ref, vext):
    vext[:, :HD] = v_ref[...]
    vext[:, HD:] = jnp.ones((v_ref.shape[0], HD), BF)
    scale = HD ** (-0.5) * math.log2(math.e)
    rows = lax.broadcasted_iota(jnp.int32, (256, 512), 0) % 128
    cols = lax.broadcasted_iota(jnp.int32, (256, 512), 1)
    behind = cols - rows
    for part in range(NX):
        length = 512 * (part + 1)
        for block in range(2):
            q = q_ref[part, block]
            q = jnp.concatenate([q[:, :HD], q[:, HD:]], axis=0)
            scores = lax.dot_general(
                q, k_ref[:length, :], (((1,), (1,)), ((), ())), preferred_element_type=F32
            )
            allowed = behind <= (s[ZH] * 2 + block) * 128
            last = jnp.where(allowed, scores[:, length - 512 :], -1e30)
            if part:
                scores = jnp.concatenate([scores[:, : length - 512], last], axis=1)
            else:
                scores = last
            top = jnp.max(scores, axis=-1, keepdims=True)
            probs = jnp.exp2((scores - top) * scale).astype(BF)
            mixed = jnp.dot(probs, vext[:length, :], preferred_element_type=F32)
            mixed = (mixed[:, :HD] / mixed[:, HD:]).astype(BF)
            at = (block * NX + part) * 128
            out_ref[at : at + 128, :HD] = mixed[:128]
            out_ref[at : at + 128, HD:] = mixed[128:]


def project_kernel(s, ctx_a, ctx_ac, ctx_b, ctx_bc, w_a, w_ac, w_z, own, o1, o2, o3, total):
    def dot(a, b):
        return jnp.dot(a[...], b, preferred_element_type=F32)

    total[...] = (
        dot(ctx_a, w_a[...])
        + dot(ctx_ac, w_ac[...])
        + dot(ctx_b, w_z[:256])
        + dot(ctx_bc, w_z[256:])
    )
    for j, out in enumerate((own, o1, o2, o3)):
        for block in range(2):
            at = pl.multiple_of((block * NX + (s[X] + j) % NX) * 128, 128)
            out[block] = total[pl.ds(at, 128), :].astype(out.dtype)


def finish_kernel(s, own, r1, r2, r3, res, res_other, *refs):
    def rows(at):
        parts = own[at] + r1[at].astype(F32) + r2[at].astype(F32) + r3[at].astype(F32)
        return parts

    same, cross = refs[-2], refs[-1]
    same[...] = (res[...].astype(F32) + rows(s[C])).astype(BF)
    cross[...] = (res_other[...].astype(F32) + rows(1 - s[C])).astype(BF)


def assemble_kernel(s, same0, same1, got0, got1, target):
    for piece, stage, core in (
        (same0, 0, s[C]),
        (same1, 1, s[C]),
        (got0, 0, 1 - s[C]),
        (got1, 1, 1 - s[C]),
    ):
        at = pl.multiple_of(((s[D] + block_of(stage, core)) % 4) * 640, 128)
        target[:, pl.ds(at, 640)] = piece[...]


def compare_kernel(stage, s, pred, normed, proj, got_same, got_cross, *refs):
    before, (gp_out, back_out, small, gp, back, sems) = refs[:-6], refs[-6:]
    if stage == 0:
        small[...] = jnp.zeros((32, 128), F32)
    else:
        small[...] = before[2][...]
    square = jnp.zeros((1, 640), F32)
    inner, starts, copies = [], [], []
    for i, (got, core) in enumerate(((got_same, s[C]), (got_cross, 1 - s[C]))):
        seq = (s[D] + 4 - block_of(stage, core)) % 4
        at = pl.multiple_of(seq * 128, 128)
        starts.append((seq, at))
        live = lax.broadcasted_iota(jnp.int32, (128, 640), 0) < s[LENGTHS + seq] - s[FIRST]
        here = pred[pl.ds(at, 128), :]
        diff = jnp.where(live, here - got[...].astype(F32), 0.0)
        square = square + jnp.sum(diff * diff, axis=0, keepdims=True)
        rounded = diff.astype(BF)
        gp[i * 128 : i * 128 + 128] = rounded
        inner.append(jnp.sum(rounded.astype(F32) * here, axis=-1, keepdims=True))
        copies.append(
            pltpu.make_async_copy(gp.at[pl.ds(i * 128, 128)], gp_out.at[pl.ds(at, 128)], sems.at[i])
        )
        copies[-1].start()
    small[20:21, :] = small[20:21, :] + jnp.sum(square, axis=-1, keepdims=True)
    turned = jnp.broadcast_to(jnp.concatenate(inner, axis=0), (256, 128)).T
    for i, (seq, _) in enumerate(starts):
        small[pl.ds(21 + seq, 1), :] = turned[:1, i * 128 : i * 128 + 128]
    for half in range(2):
        for part in range(2):
            base = half * 1280 + part * 640
            grad = lax.dot_general(
                gp[...], proj[base : base + 640, :], (((1,), (1,)), ((), ())), preferred_element_type=F32
            )
            total = jnp.zeros((128, 640), F32)
            for i, (_, at) in enumerate(starts):
                rows = grad[i * 128 : i * 128 + 128]
                back[half, i, :, part * 640 : part * 640 + 640] = rows.astype(BF)
                total = total + rows * normed[pl.ds(at, 128), base : base + 640].astype(F32)
            gain = jnp.sum(total, axis=0, keepdims=True)
            for i in range(5):
                row = base // 128 + i
                small[row : row + 1, :] = small[row : row + 1, :] + gain[:, i * 128 : i * 128 + 128]
        for i, (_, at) in enumerate(starts):
            copies.append(
                pltpu.make_async_copy(
                    back.at[half, i], back_out.at[half, pl.ds(at, 128)], sems.at[2 + half * 2 + i]
                )
            )
            copies[-1].start()
    for copy in copies:
        copy.wait()


def hidden_kernel(s, grad, inner, hidden, inverse_rms, norm_gain, out):
    scale = inverse_rms[...]
    unit = hidden[...].astype(F32) * scale
    out[...] = scale * (grad[...].astype(F32) * norm_gain[...] - unit * (inner[...] / D_S))


def gproj_kernel(s, normed, gp, sent, kept):
    first = s[C] == 0
    for part in range(NX):
        total = lax.dot_general(
            normed[:, part * 640 : part * 640 + 640],
            gp[...],
            (((0,), (0,)), ((), ())),
            preferred_element_type=F32,
        )
        for z in range(2):
            low = total[z * 320 : z * 320 + 160]
            high = total[z * 320 + 160 : z * 320 + 320]
            sent[part, z] = jnp.where(first, high, low).astype(BF)
            kept[part, z] = jnp.where(first, low, high)


def gproj_add_kernel(s, kept, recv, own, o1, o2, o3):
    for j, out in enumerate((own, o1, o2, o3)):
        at = (s[X] + j) % NX
        out[...] = (kept[at] + recv[at].astype(F32)).astype(out.dtype)


def gproj_sum_kernel(s, own, r1, r2, r3, sent, kept):
    z = s[ZH]

    def total(at):
        return own[at] + r1[at].astype(F32) + r2[at].astype(F32) + r3[at].astype(F32)

    sent[...] = total(1 - z).astype(BF)
    kept[...] = total(z)


def sum_over(array, axis, n):
    got = [lax.ppermute(array, axis, ring(n, j)) for j in range(1, n)]
    got = lax.optimization_barrier(got)
    return sum(got, array)


def body(
    queries, keys, values, out_weight, residual, student_hidden, norm_gain, projection, lengths
):
    g, d = lax.axis_index("grp"), lax.axis_index("dp")
    x, zh, c = lax.axis_index("x"), lax.axis_index("zh"), lax.axis_index("core")
    zc = zh * 2 + c
    m = x * 4 + zc
    half = D_T // 2
    blk = D_T // 8
    rows = D_S // 16
    width = D_S // 2
    barrier = lax.optimization_barrier
    scalars = Ordered(
        jnp.concatenate([jnp.stack([x, zc, g, d, zh, c, m * 128]).astype(jnp.int32), lengths])
    )
    swap = ring(2, 1)
    stages = (0, 1)

    def column(stage, near, mine, n):
        def index(i, s):
            return (0, column_block(s, stage, near, mine))

        return pl.BlockSpec((n, blk), index)

    q5 = queries.reshape(NX, 4, 128, 256)
    q_block = (NX, 2, 128, 256)
    along_z, w_out, res_out = call(
        pick_kernel,
        scalars,
        [
            (q5, pl.BlockSpec(q_block, lambda i, s: (0, 1 - s[ZH], 0, 0))),
            *[(out_weight, column(st, near, False, 256)) for near in (False, True) for st in stages],
            *[(residual[0], column(st, True, False, 128)) for st in stages],
        ],
        [(q_block, BF, True), ((256, 4 * blk), BF, True), ((128, 2 * blk), BF, True)],
        "pick",
        pinned=range(7),
    )
    along_z = lax.ppermute(along_z, ("grp", "zh"), WRAP)
    w_other = lax.ppermute(w_out, "core", swap)
    res_other = lax.ppermute(res_out, "core", swap)

    def attend(q, spec, name):
        return call(
            attend_kernel,
            scalars,
            [
                (q, spec),
                (keys[0], pl.BlockSpec((2048, HD), lambda i, s: (0, s[X]))),
                (values[0], pl.BlockSpec((2048, HD), lambda i, s: (0, s[X]))),
            ],
            [((1024, 256), BF)],
            name,
            scratch=[pltpu.VMEM((2048, 2 * HD), BF)],
            mib=40,
        )[0]

    hidden, _ = barrier((student_hidden[0], w_out))
    hidden = hidden.astype(F32)
    inverse_rms = lax.rsqrt(jnp.mean(hidden * hidden, axis=-1, keepdims=True) + 1e-06)
    normed = (hidden * inverse_rms * norm_gain).astype(BF)
    scalars.after(normed)
    normed = lax.all_gather(normed, "dp", axis=0, tiled=True)

    w_z = call(
        pick_weights_kernel,
        scalars,
        [
            *[(out_weight, column(st, False, True, 256)) for st in stages],
            (w_other, pl.BlockSpec((256, 2 * blk), lambda i, s: (0, 0))),
        ],
        [((512, blk), BF, True)] * 2,
        "pick_weights",
        pinned=range(3),
    )
    ctx_a = attend(q5, pl.BlockSpec(q_block, lambda i, s: (0, s[ZH], 0, 0)), "attend_chip")
    w_z = [lax.ppermute(w, ("grp", "zh"), WRAP) for w in w_z]
    ctx_ac = lax.ppermute(ctx_a, "core", swap)
    along_z, _ = barrier((along_z, ctx_a))
    ctx_b = attend(along_z, whole(q_block), "attend_next")
    ctx_bc = lax.ppermute(ctx_b, "core", swap)

    projected = []
    for st in stages:
        own, *outs = call(
            project_kernel,
            scalars,
            [
                *[(ctx, whole((1024, 256))) for ctx in (ctx_a, ctx_ac, ctx_b, ctx_bc)],
                (out_weight, column(st, True, True, 256)),
                (w_other, pl.BlockSpec((256, blk), lambda i, s, st=st: (0, 2 + st))),
                (w_z[st], whole((512, blk))),
            ],
            [((2, 128, blk), F32)] + [((2, 128, blk), BF, True)] * 3,
            f"project_{st}",
            scratch=[pltpu.VMEM((1024, blk), F32)],
        )
        if st == 0:
            normed, _ = barrier((normed, own))
            predicted = jnp.dot(normed, projection, preferred_element_type=F32)
            scalars.after(predicted)
        projected.append((own, {j: lax.ppermute(outs[j - 1], "x", ring(NX, j)) for j in (2, 1, 3)}))

    same, cross, arrived, written = [], [], [], ()
    for st in stages:
        own, got = projected[st]
        done_same, done_cross = call(
            finish_kernel,
            scalars,
            [
                (own, whole((2, 128, blk))),
                *[(got[j], whole((2, 128, blk))) for j in (1, 2, 3)],
                (residual[0], column(st, True, True, 128)),
                (res_other, pl.BlockSpec((128, blk), lambda i, s, st=st: (0, st))),
            ],
            [((128, blk), BF)] * 2,
            f"finish_{st}",
        )
        same.append(done_same)
        cross.append(done_cross)
        arrived.append(
            (
                lax.ppermute(done_same, ("dp", "core"), to_owner(st, False)),
                lax.ppermute(done_cross, ("dp", "core"), to_owner(st, True)),
            )
        )
    for st in stages:
        specs = (IN_HBM, IN_HBM, whole((32, 128)))
        written = call(
            functools.partial(compare_kernel, st),
            scalars,
            [
                (predicted, whole((512, blk))),
                (normed, whole((512, D_S))),
                (projection, whole((D_S, blk))),
                *[(a, whole((128, blk))) for a in arrived[st]],
                *zip(written, specs),
            ],
            [((512, blk), BF, True), ((2, 512, width), BF, True), ((32, 128), F32)],
            f"compare_{st}",
            scratch=[
                pltpu.VMEM((256, blk), BF),
                pltpu.VMEM((2, 2, 128, width), BF),
                pltpu.SemaphoreType.DMA((6,)),
            ],
            pinned=(5, 6) if st else (),
            blocked={0: IN_HBM, 1: IN_HBM},
            aliases={6: 0, 7: 1} if st else {},
        )
    gp, back, small = written
    part = (NX, 2, rows, blk)
    back = back.reshape(1024, width)
    summed = lax.psum_scatter(back, ("grp", "dp"), scatter_dimension=0, tiled=True)

    live_count = jnp.sum(lengths).astype(F32)
    sent, kept = call(
        gproj_kernel,
        scalars,
        [(normed, whole((512, D_S))), (gp, whole((512, blk)))],
        [(part, BF, True), (part, F32)],
        "gproj",
    )
    recv = lax.ppermute(sent, "core", swap)
    inner = small[21:25]
    small = sum_over(small[:21], "core", 2)
    small, _ = barrier((jnp.concatenate([small, inner]), sent))
    own, *outs = call(
        gproj_add_kernel,
        scalars,
        [(kept, whole(part)), (recv, whole(part))],
        [(part[1:], F32)] + [(part[1:], BF, True)] * 3,
        "gproj_add",
    )
    got = {j: lax.ppermute(outs[j - 1], "x", ring(NX, j)) for j in (2, 1, 3)}

    cross = [lax.ppermute(a, "core", swap) for a in barrier((*cross, own))[:2]]
    small, _ = barrier((small, own))
    small = sum_over(small, "dp", 4)
    small = sum_over(small, "grp", 2)
    inner = lax.dynamic_slice_in_dim(small, 21 + d, 1, 0)
    small = sum_over(small[:21], "zh", 2)
    (target,) = call(
        assemble_kernel,
        scalars,
        [(a, whole((128, blk))) for a in (*same, *cross)],
        [((128, half), BF)],
        "assemble",
    )
    scalars.after(small)
    gsent, gkept = call(
        gproj_sum_kernel,
        scalars,
        [(own, whole(part[1:]))] + [(got[j], whole(part[1:])) for j in (1, 2, 3)],
        [((rows, blk), BF, True), ((rows, blk), F32)],
        "gproj_sum",
    )
    gsent = lax.ppermute(gsent, "zh", swap)
    small, _ = barrier((small, gkept))
    sums = [lax.ppermute(small, "x", ring(NX, j)) for j in (1, 2, 3)]
    half_shape = (128, width)
    (grad_hidden,) = call(
        hidden_kernel,
        scalars,
        [
            (summed, whole(half_shape)),
            (inner.reshape(128, 1), whole((128, 1))),
            (student_hidden[0], pl.BlockSpec((128, width), lambda i, s: (0, s[G]))),
            (inverse_rms, whole((128, 1))),
            (norm_gain.reshape(1, D_S), pl.BlockSpec((1, width), lambda i, s: (0, s[G]))),
        ],
        [(half_shape, F32)],
        "hidden",
        pinned=range(1),
    )
    gsent, grad_hidden = barrier((gsent, grad_hidden))
    grad_proj = (gkept + gsent.astype(F32)) / live_count
    *sums, grad_proj = barrier((*sums, grad_proj))
    small = sum(sums, small)
    small = small.reshape(-1)
    distill_loss = small[20 * 128] / (live_count * D_T)
    gain_half = lax.dynamic_slice_in_dim(norm_gain, g * width, width, 0)
    grad_gain = lax.dynamic_slice_in_dim(small, g * width, width, 0) / (gain_half * live_count)
    return (target[None], distill_loss, grad_proj, grad_gain, grad_hidden[None])


def solution(mesh):
    fine = Mesh(mesh.devices.reshape(2, 4, 4, 2, 2), ("grp", "dp", "x", "zh", "core"))
    in_specs = (
        P("dp", None, MP),
        P("dp", None, None),
        P("dp", None, None),
        P(MP, None),
        P("dp", MP, None),
        P("dp", MP, None),
        P(),
        P(None, ("grp", "dp")),
        P(),
    )
    out_specs = (P("dp", MP, "grp"), P(), P(MP, ("grp", "dp")), P("grp"), P("dp", MP, "grp"))
    return jax.shard_map(body, mesh=fine, in_specs=in_specs, out_specs=out_specs, check_vma=False)
```

```python
import functools
import math

import jax
import jax.numpy as jnp
from jax import lax
from jax.experimental import pallas as pl
from jax.experimental.pallas import tpu as pltpu
from jax.sharding import Mesh
from jax.sharding import PartitionSpec as P

D_T = 5120
D_S = 2560
HD = 128
HQ = 32
KVH = 4

BF = jnp.bfloat16
F32 = jnp.float32
NX = 4
NZ = 4
MP = ("x", "zh", "core")


def ring(n, k):
    return [(i, (i + k) % n) for i in range(n)]


WRAP = [(g * 2 + z, (1 - g) * 2 + (1 - z)) for g in range(2) for z in range(2)]
MIB = 32
COST = 1
IN_HBM = pl.BlockSpec(memory_space=pltpu.HBM)


def block_of(stage, core):
    return 2 + core if stage == 0 else 1 - core


def to_owner(stage, cross):
    return [
        (d * 2 + c, (d + block_of(stage, c)) % 4 * 2 + (1 - c if cross else c))
        for d in range(4)
        for c in range(2)
    ]


def whole(shape):
    return pl.BlockSpec(shape, lambda i, s: (0,) * len(shape))


def call(kernel, scalars, ins, outs, name, scratch=(), mib=MIB, pinned=(), steps=1, blocked=None, aliases=None):
    outs = pl.pallas_call(
        kernel,
        out_shape=[
            pltpu.HBM(o[0], o[1]) if len(o) == 3 else jax.ShapeDtypeStruct(*o) for o in outs
        ],
        grid_spec=pltpu.PrefetchScalarGridSpec(
            num_scalar_prefetch=1,
            grid=(steps,),
            in_specs=[spec for _, spec in ins],
            out_specs=[(blocked or {}).get(i, whole(o[0])) for i, o in enumerate(outs)],
            scratch_shapes=list(scratch),
        ),
        compiler_params=pltpu.CompilerParams(vmem_limit_bytes=mib * 1024 * 1024),
        cost_estimate=pl.CostEstimate(flops=COST, bytes_accessed=COST, transcendentals=0),
        input_output_aliases=aliases or {},
        name=name,
    )(scalars.value, *[
            pltpu.with_memory_space_constraint(a, pltpu.HBM) if i in pinned else a
            for i, (a, _) in enumerate(ins)
        ])
    scalars.after(outs[0])
    return outs


class Ordered:
    def __init__(self, value):
        self.value = value

    def after(self, array):
        self.value, _ = lax.optimization_barrier((self.value, array))


X, ZC, G, D, ZH, C, FIRST, LENGTHS = range(8)


def column_block(s, stage, near, mine):
    core = s[C] if mine else 1 - s[C]
    side = s[G] if near else 1 - s[G]
    return side * 4 + (s[D] + block_of(stage, core)) % 4


def pick_kernel(s, q, w0, w1, w2, w3, res0, res1, q_out, w_out, res_out):
    q_out[...] = q[...]
    for i, w in enumerate((w0, w1, w2, w3)):
        w_out[:, i * 640 : i * 640 + 640] = w[...]
    res_out[:, :640] = res0[...]
    res_out[:, 640:] = res1[...]


def pick_weights_kernel(s, own0, own1, other, out0, out1):
    for i, (own, out) in enumerate(((own0, out0), (own1, out1))):
        out[:256] = own[...]
        out[256:] = other[:, i * 640 : i * 640 + 640]


def attend_kernel(s, q_ref, k_ref, v_ref, out_ref, vext):
    vext[:, :HD] = v_ref[...]
    vext[:, HD:] = jnp.ones((v_ref.shape[0], HD), BF)
    scale = HD ** (-0.5) * math.log2(math.e)
    rows = lax.broadcasted_iota(jnp.int32, (256, 512), 0) % 128
    cols = lax.broadcasted_iota(jnp.int32, (256, 512), 1)
    behind = cols - rows
    for part in range(NX):
        length = 512 * (part + 1)
        for block in range(2):
            q = q_ref[part, block]
            q = jnp.concatenate([q[:, :HD], q[:, HD:]], axis=0)
            scores = lax.dot_general(
                q, k_ref[:length, :], (((1,), (1,)), ((), ())), preferred_element_type=F32
            )
            allowed = behind <= (s[ZH] * 2 + block) * 128
            last = jnp.where(allowed, scores[:, length - 512 :], -1e30)
            if part:
                scores = jnp.concatenate([scores[:, : length - 512], last], axis=1)
            else:
                scores = last
            top = jnp.max(scores, axis=-1, keepdims=True)
            probs = jnp.exp2((scores - top) * scale).astype(BF)
            mixed = jnp.dot(probs, vext[:length, :], preferred_element_type=F32)
            mixed = (mixed[:, :HD] / mixed[:, HD:]).astype(BF)
            at = (block * NX + part) * 128
            out_ref[at : at + 128, :HD] = mixed[:128]
            out_ref[at : at + 128, HD:] = mixed[128:]


def project_kernel(s, ctx_a, ctx_ac, ctx_b, ctx_bc, w_a, w_ac, w_z, own, o1, o2, o3, total):
    def dot(a, b):
        return jnp.dot(a[...], b, preferred_element_type=F32)

    total[...] = (
        dot(ctx_a, w_a[...])
        + dot(ctx_ac, w_ac[...])
        + dot(ctx_b, w_z[:256])
        + dot(ctx_bc, w_z[256:])
    )
    for j, out in enumerate((own, o1, o2, o3)):
        for block in range(2):
            at = pl.multiple_of((block * NX + (s[X] + j) % NX) * 128, 128)
            out[block] = total[pl.ds(at, 128), :].astype(out.dtype)


def finish_kernel(s, own, r1, r2, r3, res, res_other, *refs):
    def rows(at):
        parts = own[at] + r1[at].astype(F32) + r2[at].astype(F32) + r3[at].astype(F32)
        return parts

    same, cross = refs[-2], refs[-1]
    same[...] = (res[...].astype(F32) + rows(s[C])).astype(BF)
    cross[...] = (res_other[...].astype(F32) + rows(1 - s[C])).astype(BF)


def assemble_kernel(s, same0, same1, got0, got1, target):
    for piece, stage, core in (
        (same0, 0, s[C]),
        (same1, 1, s[C]),
        (got0, 0, 1 - s[C]),
        (got1, 1, 1 - s[C]),
    ):
        at = pl.multiple_of(((s[D] + block_of(stage, core)) % 4) * 640, 128)
        target[:, pl.ds(at, 640)] = piece[...]


def compare_kernel(stage, s, pred, normed, proj, got_same, got_cross, *refs):
    before, (gp_out, back_out, small, gp, back, sems) = refs[:-6], refs[-6:]
    if stage == 0:
        small[...] = jnp.zeros((32, 128), F32)
    else:
        small[...] = before[2][...]
    square = jnp.zeros((1, 640), F32)
    inner, starts, copies = [], [], []
    for i, (got, core) in enumerate(((got_same, s[C]), (got_cross, 1 - s[C]))):
        seq = (s[D] + 4 - block_of(stage, core)) % 4
        at = pl.multiple_of(seq * 128, 128)
        starts.append((seq, at))
        live = lax.broadcasted_iota(jnp.int32, (128, 640), 0) < s[LENGTHS + seq] - s[FIRST]
        here = pred[pl.ds(at, 128), :]
        diff = jnp.where(live, here - got[...].astype(F32), 0.0)
        square = square + jnp.sum(diff * diff, axis=0, keepdims=True)
        rounded = diff.astype(BF)
        gp[i * 128 : i * 128 + 128] = rounded
        inner.append(jnp.sum(rounded.astype(F32) * here, axis=-1, keepdims=True))
        copies.append(
            pltpu.make_async_copy(gp.at[pl.ds(i * 128, 128)], gp_out.at[pl.ds(at, 128)], sems.at[i])
        )
        copies[-1].start()
    small[20:21, :] = small[20:21, :] + jnp.sum(square, axis=-1, keepdims=True)
    turned = jnp.broadcast_to(jnp.concatenate(inner, axis=0), (256, 128)).T
    for i, (seq, _) in enumerate(starts):
        small[pl.ds(21 + seq, 1), :] = turned[:1, i * 128 : i * 128 + 128]
    for half in range(2):
        for part in range(2):
            base = half * 1280 + part * 640
            grad = lax.dot_general(
                gp[...], proj[base : base + 640, :], (((1,), (1,)), ((), ())), preferred_element_type=F32
            )
            total = jnp.zeros((128, 640), F32)
            for i, (_, at) in enumerate(starts):
                rows = grad[i * 128 : i * 128 + 128]
                back[half, i, :, part * 640 : part * 640 + 640] = rows.astype(BF)
                total = total + rows * normed[pl.ds(at, 128), base : base + 640].astype(F32)
            gain = jnp.sum(total, axis=0, keepdims=True)
            for i in range(5):
                row = base // 128 + i
                small[row : row + 1, :] = small[row : row + 1, :] + gain[:, i * 128 : i * 128 + 128]
        for i, (_, at) in enumerate(starts):
            copies.append(
                pltpu.make_async_copy(
                    back.at[half, i], back_out.at[half, pl.ds(at, 128)], sems.at[2 + half * 2 + i]
                )
            )
            copies[-1].start()
    for copy in copies:
        copy.wait()


def hidden_kernel(s, grad, inner, hidden, inverse_rms, norm_gain, out):
    scale = inverse_rms[...]
    unit = hidden[...].astype(F32) * scale
    mean_term = jnp.broadcast_to(inner[...], (128, 128)).T[:, :1] / D_S
    out[...] = scale * (grad[...].astype(F32) * norm_gain[...] - unit * mean_term)


def gproj_kernel(s, normed, gp, sent, kept):
    first = s[C] == 0
    for part in range(NX):
        total = lax.dot_general(
            normed[:, part * 640 : part * 640 + 640],
            gp[...],
            (((0,), (0,)), ((), ())),
            preferred_element_type=F32,
        )
        for z in range(2):
            low = total[z * 320 : z * 320 + 160]
            high = total[z * 320 + 160 : z * 320 + 320]
            sent[part, z] = jnp.where(first, high, low).astype(BF)
            kept[part, z] = jnp.where(first, low, high)


def gproj_add_kernel(s, kept, recv, own, o1, o2, o3):
    for j, out in enumerate((own, o1, o2, o3)):
        at = (s[X] + j) % NX
        out[...] = (kept[at] + recv[at].astype(F32)).astype(out.dtype)


def gproj_sum_kernel(s, own, r1, r2, r3, sent, kept):
    z = s[ZH]

    def total(at):
        return own[at] + r1[at].astype(F32) + r2[at].astype(F32) + r3[at].astype(F32)

    sent[...] = total(1 - z).astype(BF)
    kept[...] = total(z)


def sum_over(array, axis, n):
    got = [lax.ppermute(array, axis, ring(n, j)) for j in range(1, n)]
    got = lax.optimization_barrier(got)
    return sum(got, array)


def body(
    queries, keys, values, out_weight, residual, student_hidden, norm_gain, projection, lengths
):
    g, d = lax.axis_index("grp"), lax.axis_index("dp")
    x, zh, c = lax.axis_index("x"), lax.axis_index("zh"), lax.axis_index("core")
    zc = zh * 2 + c
    m = x * 4 + zc
    half = D_T // 2
    blk = D_T // 8
    rows = D_S // 16
    width = D_S // 2
    barrier = lax.optimization_barrier
    scalars = Ordered(
        jnp.concatenate([jnp.stack([x, zc, g, d, zh, c, m * 128]).astype(jnp.int32), lengths])
    )
    swap = ring(2, 1)
    stages = (0, 1)

    def column(stage, near, mine, n):
        def index(i, s):
            return (0, column_block(s, stage, near, mine))

        return pl.BlockSpec((n, blk), index)

    q5 = queries.reshape(NX, 4, 128, 256)
    q_block = (NX, 2, 128, 256)
    along_z, w_out, res_out = call(
        pick_kernel,
        scalars,
        [
            (q5, pl.BlockSpec(q_block, lambda i, s: (0, 1 - s[ZH], 0, 0))),
            *[(out_weight, column(st, near, False, 256)) for near in (False, True) for st in stages],
            *[(residual[0], column(st, True, False, 128)) for st in stages],
        ],
        [(q_block, BF, True), ((256, 4 * blk), BF, True), ((128, 2 * blk), BF, True)],
        "pick",
        pinned=range(7),
    )
    along_z = lax.ppermute(along_z, ("grp", "zh"), WRAP)
    w_other = lax.ppermute(w_out, "core", swap)
    res_other = lax.ppermute(res_out, "core", swap)

    def attend(q, spec, name):
        return call(
            attend_kernel,
            scalars,
            [
                (q, spec),
                (keys[0], pl.BlockSpec((2048, HD), lambda i, s: (0, s[X]))),
                (values[0], pl.BlockSpec((2048, HD), lambda i, s: (0, s[X]))),
            ],
            [((1024, 256), BF)],
            name,
            scratch=[pltpu.VMEM((2048, 2 * HD), BF)],
            mib=40,
        )[0]

    hidden, _ = barrier((student_hidden[0], w_out))
    hidden = hidden.astype(F32)
    inverse_rms = lax.rsqrt(jnp.mean(hidden * hidden, axis=-1, keepdims=True) + 1e-06)
    normed = (hidden * inverse_rms * norm_gain).astype(BF)
    scalars.after(normed)
    normed = lax.all_gather(normed, "dp", axis=0, tiled=True)

    w_z = call(
        pick_weights_kernel,
        scalars,
        [
            *[(out_weight, column(st, False, True, 256)) for st in stages],
            (w_other, pl.BlockSpec((256, 2 * blk), lambda i, s: (0, 0))),
        ],
        [((512, blk), BF, True)] * 2,
        "pick_weights",
        pinned=range(3),
    )
    ctx_a = attend(q5, pl.BlockSpec(q_block, lambda i, s: (0, s[ZH], 0, 0)), "attend_chip")
    w_z = [lax.ppermute(w, ("grp", "zh"), WRAP) for w in w_z]
    ctx_ac = lax.ppermute(ctx_a, "core", swap)
    along_z, _ = barrier((along_z, ctx_a))
    ctx_b = attend(along_z, whole(q_block), "attend_next")
    ctx_bc = lax.ppermute(ctx_b, "core", swap)

    projected = []
    for st in stages:
        own, *outs = call(
            project_kernel,
            scalars,
            [
                *[(ctx, whole((1024, 256))) for ctx in (ctx_a, ctx_ac, ctx_b, ctx_bc)],
                (out_weight, column(st, True, True, 256)),
                (w_other, pl.BlockSpec((256, blk), lambda i, s, st=st: (0, 2 + st))),
                (w_z[st], whole((512, blk))),
            ],
            [((2, 128, blk), F32)] + [((2, 128, blk), BF, True)] * 3,
            f"project_{st}",
            scratch=[pltpu.VMEM((1024, blk), F32)],
        )
        if st == 0:
            normed, _ = barrier((normed, own))
            predicted = jnp.dot(normed, projection, preferred_element_type=F32)
            scalars.after(predicted)
        projected.append((own, {j: lax.ppermute(outs[j - 1], "x", ring(NX, j)) for j in (2, 1, 3)}))

    same, cross, arrived, written = [], [], [], ()
    for st in stages:
        own, got = projected[st]
        done_same, done_cross = call(
            finish_kernel,
            scalars,
            [
                (own, whole((2, 128, blk))),
                *[(got[j], whole((2, 128, blk))) for j in (1, 2, 3)],
                (residual[0], column(st, True, True, 128)),
                (res_other, pl.BlockSpec((128, blk), lambda i, s, st=st: (0, st))),
            ],
            [((128, blk), BF)] * 2,
            f"finish_{st}",
        )
        same.append(done_same)
        cross.append(done_cross)
        arrived.append(
            (
                lax.ppermute(done_same, ("dp", "core"), to_owner(st, False)),
                lax.ppermute(done_cross, ("dp", "core"), to_owner(st, True)),
            )
        )
    for st in stages:
        specs = (IN_HBM, IN_HBM, whole((32, 128)))
        written = call(
            functools.partial(compare_kernel, st),
            scalars,
            [
                (predicted, whole((512, blk))),
                (normed, whole((512, D_S))),
                (projection, whole((D_S, blk))),
                *[(a, whole((128, blk))) for a in arrived[st]],
                *zip(written, specs),
            ],
            [((512, blk), BF, True), ((2, 512, width), BF, True), ((32, 128), F32)],
            f"compare_{st}",
            scratch=[
                pltpu.VMEM((256, blk), BF),
                pltpu.VMEM((2, 2, 128, width), BF),
                pltpu.SemaphoreType.DMA((6,)),
            ],
            pinned=(5, 6) if st else (),
            blocked={0: IN_HBM, 1: IN_HBM},
            aliases={6: 0, 7: 1} if st else {},
        )
    gp, back, small = written
    part = (NX, 2, rows, blk)
    back = back.reshape(1024, width)
    summed = lax.psum_scatter(back, ("grp", "dp"), scatter_dimension=0, tiled=True)

    live_count = jnp.sum(lengths).astype(F32)
    sent, kept = call(
        gproj_kernel,
        scalars,
        [(normed, whole((512, D_S))), (gp, whole((512, blk)))],
        [(part, BF, True), (part, F32)],
        "gproj",
    )
    recv = lax.ppermute(sent, "core", swap)
    inner = small[21:25]
    small = sum_over(small[:21], "core", 2)
    small, _ = barrier((jnp.concatenate([small, inner]), sent))
    own, *outs = call(
        gproj_add_kernel,
        scalars,
        [(kept, whole(part)), (recv, whole(part))],
        [(part[1:], F32)] + [(part[1:], BF, True)] * 3,
        "gproj_add",
    )
    got = {j: lax.ppermute(outs[j - 1], "x", ring(NX, j)) for j in (2, 1, 3)}

    cross = [lax.ppermute(a, "core", swap) for a in barrier((*cross, own))[:2]]
    small, _ = barrier((small, own))
    small = sum_over(small, "dp", 4)
    small = sum_over(small, "grp", 2)
    inner = lax.dynamic_slice_in_dim(small, 21 + d, 1, 0)
    small = sum_over(small[:21], "zh", 2)
    (target,) = call(
        assemble_kernel,
        scalars,
        [(a, whole((128, blk))) for a in (*same, *cross)],
        [((128, half), BF)],
        "assemble",
    )
    scalars.after(small)
    gsent, gkept = call(
        gproj_sum_kernel,
        scalars,
        [(own, whole(part[1:]))] + [(got[j], whole(part[1:])) for j in (1, 2, 3)],
        [((rows, blk), BF, True), ((rows, blk), F32)],
        "gproj_sum",
    )
    gsent = lax.ppermute(gsent, "zh", swap)
    small, _ = barrier((small, gkept))
    sums = [lax.ppermute(small, "x", ring(NX, j)) for j in (1, 2, 3)]
    half_shape = (128, width)
    (grad_hidden,) = call(
        hidden_kernel,
        scalars,
        [
            (summed, whole(half_shape)),
            (inner, whole((1, 128))),
            (student_hidden[0], pl.BlockSpec((128, width), lambda i, s: (0, s[G]))),
            (inverse_rms, whole((128, 1))),
            (norm_gain.reshape(1, D_S), pl.BlockSpec((1, width), lambda i, s: (0, s[G]))),
        ],
        [(half_shape, F32)],
        "hidden",
        pinned=range(1),
    )
    gsent, grad_hidden = barrier((gsent, grad_hidden))
    grad_proj = (gkept + gsent.astype(F32)) / live_count
    *sums, grad_proj = barrier((*sums, grad_proj))
    small = sum(sums, small)
    distill_loss = small[20, 0] / (live_count * D_T)
    gain_rows = lax.dynamic_slice_in_dim(norm_gain.reshape(20, 128), g * 10, 10, 0)
    gain_sums = lax.dynamic_slice_in_dim(small, g * 10, 10, 0)
    grad_gain = (gain_sums / (gain_rows * live_count)).reshape(width)
    return (target[None], distill_loss, grad_proj, grad_gain, grad_hidden[None])


def solution(mesh):
    fine = Mesh(mesh.devices.reshape(2, 4, 4, 2, 2), ("grp", "dp", "x", "zh", "core"))
    in_specs = (
        P("dp", None, MP),
        P("dp", None, None),
        P("dp", None, None),
        P(MP, None),
        P("dp", MP, None),
        P("dp", MP, None),
        P(),
        P(None, ("grp", "dp")),
        P(),
    )
    out_specs = (P("dp", MP, "grp"), P(), P(MP, ("grp", "dp")), P("grp"), P("dp", MP, "grp"))
    return jax.shard_map(body, mesh=fine, in_specs=in_specs, out_specs=out_specs, check_vma=False)
```

```python
import functools
import math

import jax
import jax.numpy as jnp
from jax import lax
from jax.experimental import pallas as pl
from jax.experimental.pallas import tpu as pltpu
from jax.sharding import Mesh
from jax.sharding import PartitionSpec as P

D_T = 5120
D_S = 2560
HD = 128
HQ = 32
KVH = 4

BF = jnp.bfloat16
F32 = jnp.float32
NX = 4
NZ = 4
MP = ("x", "zh", "core")


def ring(n, k):
    return [(i, (i + k) % n) for i in range(n)]


WRAP = [(g * 2 + z, (1 - g) * 2 + (1 - z)) for g in range(2) for z in range(2)]
MIB = 28
COST = 1
IN_HBM = pl.BlockSpec(memory_space=pltpu.HBM)


def block_of(stage, core):
    return 2 + core if stage == 0 else 1 - core


def to_owner(stage, cross):
    return [
        (d * 2 + c, (d + block_of(stage, c)) % 4 * 2 + (1 - c if cross else c))
        for d in range(4)
        for c in range(2)
    ]


def whole(shape):
    return pl.BlockSpec(shape, lambda i, s: (0,) * len(shape))


def call(kernel, scalars, ins, outs, name, scratch=(), mib=MIB, pinned=(), steps=1, blocked=None, aliases=None):
    outs = pl.pallas_call(
        kernel,
        out_shape=[
            pltpu.HBM(o[0], o[1]) if len(o) == 3 else jax.ShapeDtypeStruct(*o) for o in outs
        ],
        grid_spec=pltpu.PrefetchScalarGridSpec(
            num_scalar_prefetch=1,
            grid=(steps,),
            in_specs=[spec for _, spec in ins],
            out_specs=[(blocked or {}).get(i, whole(o[0])) for i, o in enumerate(outs)],
            scratch_shapes=list(scratch),
        ),
        compiler_params=pltpu.CompilerParams(vmem_limit_bytes=mib * 1024 * 1024),
        cost_estimate=pl.CostEstimate(flops=COST, bytes_accessed=COST, transcendentals=0),
        input_output_aliases=aliases or {},
        name=name,
    )(scalars.value, *[
            pltpu.with_memory_space_constraint(a, pltpu.HBM) if i in pinned else a
            for i, (a, _) in enumerate(ins)
        ])
    scalars.after(outs[0])
    return outs


class Ordered:
    def __init__(self, value):
        self.value = value

    def after(self, array):
        self.value, _ = lax.optimization_barrier((self.value, array))


X, ZC, G, D, ZH, C, FIRST, LENGTHS = range(8)


def column_block(s, stage, near, mine):
    core = s[C] if mine else 1 - s[C]
    side = s[G] if near else 1 - s[G]
    return side * 4 + (s[D] + block_of(stage, core)) % 4


def pick_kernel(s, q, w0, w1, w2, w3, res0, res1, q_out, w_out, res_out):
    q_out[...] = q[...]
    for i, w in enumerate((w0, w1, w2, w3)):
        w_out[:, i * 640 : i * 640 + 640] = w[...]
    res_out[:, :640] = res0[...]
    res_out[:, 640:] = res1[...]


def pick_weights_kernel(s, own0, own1, other, out0, out1):
    for i, (own, out) in enumerate(((own0, out0), (own1, out1))):
        out[:256] = own[...]
        out[256:] = other[:, i * 640 : i * 640 + 640]


def attend_kernel(s, q_ref, k_ref, v_ref, out_ref, vext):
    vext[:, :HD] = v_ref[...]
    vext[:, HD:] = jnp.ones((v_ref.shape[0], HD), BF)
    scale = HD ** (-0.5) * math.log2(math.e)
    rows = lax.broadcasted_iota(jnp.int32, (256, 512), 0) % 128
    cols = lax.broadcasted_iota(jnp.int32, (256, 512), 1)
    behind = cols - rows
    for part in range(NX):
        length = 512 * (part + 1)
        for block in range(2):
            q = q_ref[part, block]
            q = jnp.concatenate([q[:, :HD], q[:, HD:]], axis=0)
            scores = lax.dot_general(
                q, k_ref[:length, :], (((1,), (1,)), ((), ())), preferred_element_type=F32
            )
            allowed = behind <= (s[ZH] * 2 + block) * 128
            last = jnp.where(allowed, scores[:, length - 512 :], -1e30)
            if part:
                scores = jnp.concatenate([scores[:, : length - 512], last], axis=1)
            else:
                scores = last
            top = jnp.max(scores, axis=-1, keepdims=True)
            probs = jnp.exp2((scores - top) * scale).astype(BF)
            mixed = jnp.dot(probs, vext[:length, :], preferred_element_type=F32)
            mixed = (mixed[:, :HD] / mixed[:, HD:]).astype(BF)
            at = (block * NX + part) * 128
            out_ref[at : at + 128, :HD] = mixed[:128]
            out_ref[at : at + 128, HD:] = mixed[128:]


def project_kernel(s, ctx_a, ctx_ac, ctx_b, ctx_bc, w_a, w_ac, w_z, own, o1, o2, o3, total):
    def dot(a, b):
        return jnp.dot(a[...], b, preferred_element_type=F32)

    total[...] = (
        dot(ctx_a, w_a[...])
        + dot(ctx_ac, w_ac[...])
        + dot(ctx_b, w_z[:256])
        + dot(ctx_bc, w_z[256:])
    )
    for j, out in enumerate((own, o1, o2, o3)):
        for block in range(2):
            at = pl.multiple_of((block * NX + (s[X] + j) % NX) * 128, 128)
            out[block] = total[pl.ds(at, 128), :].astype(out.dtype)


def finish_kernel(s, own, r1, r2, r3, res, res_other, *refs):
    def rows(at):
        parts = own[at] + r1[at].astype(F32) + r2[at].astype(F32) + r3[at].astype(F32)
        return parts

    same, cross = refs[-2], refs[-1]
    same[...] = (res[...].astype(F32) + rows(s[C])).astype(BF)
    cross[...] = (res_other[...].astype(F32) + rows(1 - s[C])).astype(BF)


def assemble_kernel(s, same0, same1, got0, got1, target):
    for piece, stage, core in (
        (same0, 0, s[C]),
        (same1, 1, s[C]),
        (got0, 0, 1 - s[C]),
        (got1, 1, 1 - s[C]),
    ):
        at = pl.multiple_of(((s[D] + block_of(stage, core)) % 4) * 640, 128)
        target[:, pl.ds(at, 640)] = piece[...]


def compare_kernel(stage, s, pred, normed, proj, got_same, got_cross, *refs):
    before, (gp_out, back_out, small, gp, back, sems) = refs[:-6], refs[-6:]
    if stage == 0:
        small[...] = jnp.zeros((32, 128), F32)
    else:
        small[...] = before[2][...]
    square = jnp.zeros((1, 640), F32)
    inner, starts, copies = [], [], []
    for i, (got, core) in enumerate(((got_same, s[C]), (got_cross, 1 - s[C]))):
        seq = (s[D] + 4 - block_of(stage, core)) % 4
        at = pl.multiple_of(seq * 128, 128)
        starts.append((seq, at))
        live = lax.broadcasted_iota(jnp.int32, (128, 640), 0) < s[LENGTHS + seq] - s[FIRST]
        here = pred[pl.ds(at, 128), :]
        diff = jnp.where(live, here - got[...].astype(F32), 0.0)
        square = square + jnp.sum(diff * diff, axis=0, keepdims=True)
        rounded = diff.astype(BF)
        gp[i * 128 : i * 128 + 128] = rounded
        inner.append(jnp.sum(rounded.astype(F32) * here, axis=-1, keepdims=True))
        copies.append(
            pltpu.make_async_copy(gp.at[pl.ds(i * 128, 128)], gp_out.at[pl.ds(at, 128)], sems.at[i])
        )
        copies[-1].start()
    small[20:21, :] = small[20:21, :] + jnp.sum(square, axis=-1, keepdims=True)
    turned = jnp.broadcast_to(jnp.concatenate(inner, axis=0), (256, 128)).T
    for i, (seq, _) in enumerate(starts):
        small[pl.ds(21 + seq, 1), :] = turned[:1, i * 128 : i * 128 + 128]
    for half in range(2):
        for part in range(2):
            base = half * 1280 + part * 640
            grad = lax.dot_general(
                gp[...], proj[base : base + 640, :], (((1,), (1,)), ((), ())), preferred_element_type=F32
            )
            total = jnp.zeros((128, 640), F32)
            for i, (_, at) in enumerate(starts):
                rows = grad[i * 128 : i * 128 + 128]
                back[half, i, :, part * 640 : part * 640 + 640] = rows.astype(BF)
                total = total + rows * normed[pl.ds(at, 128), base : base + 640].astype(F32)
            gain = jnp.sum(total, axis=0, keepdims=True)
            for i in range(5):
                row = base // 128 + i
                small[row : row + 1, :] = small[row : row + 1, :] + gain[:, i * 128 : i * 128 + 128]
        for i, (_, at) in enumerate(starts):
            copies.append(
                pltpu.make_async_copy(
                    back.at[half, i], back_out.at[half, pl.ds(at, 128)], sems.at[2 + half * 2 + i]
                )
            )
            copies[-1].start()
    for copy in copies:
        copy.wait()


def hidden_kernel(s, grad, inner, hidden, inverse_rms, norm_gain, out):
    scale = inverse_rms[...]
    unit = hidden[...].astype(F32) * scale
    mean_term = jnp.broadcast_to(inner[...], (128, 128)).T[:, :1] / D_S
    out[...] = scale * (grad[...].astype(F32) * norm_gain[...] - unit * mean_term)


def gproj_kernel(s, normed, gp, sent, kept):
    first = s[C] == 0
    for part in range(NX):
        total = lax.dot_general(
            normed[:, part * 640 : part * 640 + 640],
            gp[...],
            (((0,), (0,)), ((), ())),
            preferred_element_type=F32,
        )
        for z in range(2):
            low = total[z * 320 : z * 320 + 160]
            high = total[z * 320 + 160 : z * 320 + 320]
            sent[part, z] = jnp.where(first, high, low).astype(BF)
            kept[part, z] = jnp.where(first, low, high)


def gproj_add_kernel(s, kept, recv, own, o1, o2, o3):
    for j, out in enumerate((own, o1, o2, o3)):
        at = (s[X] + j) % NX
        out[...] = (kept[at] + recv[at].astype(F32)).astype(out.dtype)


def gproj_sum_kernel(s, own, r1, r2, r3, sent, kept):
    z = s[ZH]

    def total(at):
        return own[at] + r1[at].astype(F32) + r2[at].astype(F32) + r3[at].astype(F32)

    sent[...] = total(1 - z).astype(BF)
    kept[...] = total(z)


def sum_over(array, axis, n):
    got = [lax.ppermute(array, axis, ring(n, j)) for j in range(1, n)]
    got = lax.optimization_barrier(got)
    return sum(got, array)


def body(
    queries, keys, values, out_weight, residual, student_hidden, norm_gain, projection, lengths
):
    g, d = lax.axis_index("grp"), lax.axis_index("dp")
    x, zh, c = lax.axis_index("x"), lax.axis_index("zh"), lax.axis_index("core")
    zc = zh * 2 + c
    m = x * 4 + zc
    half = D_T // 2
    blk = D_T // 8
    rows = D_S // 16
    width = D_S // 2
    barrier = lax.optimization_barrier
    scalars = Ordered(
        jnp.concatenate([jnp.stack([x, zc, g, d, zh, c, m * 128]).astype(jnp.int32), lengths])
    )
    swap = ring(2, 1)
    stages = (0, 1)

    def column(stage, near, mine, n):
        def index(i, s):
            return (0, column_block(s, stage, near, mine))

        return pl.BlockSpec((n, blk), index)

    q5 = queries.reshape(NX, 4, 128, 256)
    q_block = (NX, 2, 128, 256)
    along_z, w_out, res_out = call(
        pick_kernel,
        scalars,
        [
            (q5, pl.BlockSpec(q_block, lambda i, s: (0, 1 - s[ZH], 0, 0))),
            *[(out_weight, column(st, near, False, 256)) for near in (False, True) for st in stages],
            *[(residual[0], column(st, True, False, 128)) for st in stages],
        ],
        [(q_block, BF, True), ((256, 4 * blk), BF, True), ((128, 2 * blk), BF, True)],
        "pick",
        pinned=range(7),
    )
    along_z = lax.ppermute(along_z, ("grp", "zh"), WRAP)
    w_other = lax.ppermute(w_out, "core", swap)
    res_other = lax.ppermute(res_out, "core", swap)

    def attend(q, spec, name):
        return call(
            attend_kernel,
            scalars,
            [
                (q, spec),
                (keys[0], pl.BlockSpec((2048, HD), lambda i, s: (0, s[X]))),
                (values[0], pl.BlockSpec((2048, HD), lambda i, s: (0, s[X]))),
            ],
            [((1024, 256), BF)],
            name,
            scratch=[pltpu.VMEM((2048, 2 * HD), BF)],
            mib=32,
        )[0]

    hidden, _ = barrier((student_hidden[0], w_out))
    hidden = hidden.astype(F32)
    inverse_rms = lax.rsqrt(jnp.mean(hidden * hidden, axis=-1, keepdims=True) + 1e-06)
    normed = (hidden * inverse_rms * norm_gain).astype(BF)
    scalars.after(normed)
    normed = lax.all_gather(normed, "dp", axis=0, tiled=True)

    w_z = call(
        pick_weights_kernel,
        scalars,
        [
            *[(out_weight, column(st, False, True, 256)) for st in stages],
            (w_other, pl.BlockSpec((256, 2 * blk), lambda i, s: (0, 0))),
        ],
        [((512, blk), BF, True)] * 2,
        "pick_weights",
        pinned=range(3),
    )
    ctx_a = attend(q5, pl.BlockSpec(q_block, lambda i, s: (0, s[ZH], 0, 0)), "attend_chip")
    w_z = [lax.ppermute(w, ("grp", "zh"), WRAP) for w in w_z]
    ctx_ac = lax.ppermute(ctx_a, "core", swap)
    along_z, _ = barrier((along_z, ctx_a))
    ctx_b = attend(along_z, whole(q_block), "attend_next")
    ctx_bc = lax.ppermute(ctx_b, "core", swap)

    projected = []
    for st in stages:
        own, *outs = call(
            project_kernel,
            scalars,
            [
                *[(ctx, whole((1024, 256))) for ctx in (ctx_a, ctx_ac, ctx_b, ctx_bc)],
                (out_weight, column(st, True, True, 256)),
                (w_other, pl.BlockSpec((256, blk), lambda i, s, st=st: (0, 2 + st))),
                (w_z[st], whole((512, blk))),
            ],
            [((2, 128, blk), F32)] + [((2, 128, blk), BF, True)] * 3,
            f"project_{st}",
            scratch=[pltpu.VMEM((1024, blk), F32)],
        )
        if st == 0:
            normed, _ = barrier((normed, own))
            predicted = jnp.dot(normed, projection, preferred_element_type=F32)
            scalars.after(predicted)
        projected.append((own, {j: lax.ppermute(outs[j - 1], "x", ring(NX, j)) for j in (2, 1, 3)}))

    same, cross, arrived, written = [], [], [], ()
    for st in stages:
        own, got = projected[st]
        done_same, done_cross = call(
            finish_kernel,
            scalars,
            [
                (own, whole((2, 128, blk))),
                *[(got[j], whole((2, 128, blk))) for j in (1, 2, 3)],
                (residual[0], column(st, True, True, 128)),
                (res_other, pl.BlockSpec((128, blk), lambda i, s, st=st: (0, st))),
            ],
            [((128, blk), BF)] * 2,
            f"finish_{st}",
        )
        same.append(done_same)
        cross.append(done_cross)
        arrived.append(
            (
                lax.ppermute(done_same, ("dp", "core"), to_owner(st, False)),
                lax.ppermute(done_cross, ("dp", "core"), to_owner(st, True)),
            )
        )
    for st in stages:
        specs = (IN_HBM, IN_HBM, whole((32, 128)))
        written = call(
            functools.partial(compare_kernel, st),
            scalars,
            [
                (predicted, whole((512, blk))),
                (normed, whole((512, D_S))),
                (projection, whole((D_S, blk))),
                *[(a, whole((128, blk))) for a in arrived[st]],
                *zip(written, specs),
            ],
            [((512, blk), BF, True), ((2, 512, width), BF, True), ((32, 128), F32)],
            f"compare_{st}",
            scratch=[
                pltpu.VMEM((256, blk), BF),
                pltpu.VMEM((2, 2, 128, width), BF),
                pltpu.SemaphoreType.DMA((6,)),
            ],
            pinned=(5, 6) if st else (),
            blocked={0: IN_HBM, 1: IN_HBM},
            aliases={6: 0, 7: 1} if st else {},
        )
    gp, back, small = written
    part = (NX, 2, rows, blk)
    back = back.reshape(1024, width)
    summed = lax.psum_scatter(back, ("grp", "dp"), scatter_dimension=0, tiled=True)

    live_count = jnp.sum(lengths).astype(F32)
    sent, kept = call(
        gproj_kernel,
        scalars,
        [(normed, whole((512, D_S))), (gp, whole((512, blk)))],
        [(part, BF, True), (part, F32)],
        "gproj",
    )
    recv = lax.ppermute(sent, "core", swap)
    inner = small[21:25]
    small = sum_over(small[:21], "core", 2)
    small, _ = barrier((jnp.concatenate([small, inner]), sent))
    own, *outs = call(
        gproj_add_kernel,
        scalars,
        [(kept, whole(part)), (recv, whole(part))],
        [(part[1:], F32)] + [(part[1:], BF, True)] * 3,
        "gproj_add",
    )
    got = {j: lax.ppermute(outs[j - 1], "x", ring(NX, j)) for j in (2, 1, 3)}

    cross = [lax.ppermute(a, "core", swap) for a in barrier((*cross, own))[:2]]
    small, _ = barrier((small, own))
    small = sum_over(small, "dp", 4)
    small = sum_over(small, "grp", 2)
    inner = lax.dynamic_slice_in_dim(small, 21 + d, 1, 0)
    small = sum_over(small[:21], "zh", 2)
    (target,) = call(
        assemble_kernel,
        scalars,
        [(a, whole((128, blk))) for a in (*same, *cross)],
        [((128, half), BF)],
        "assemble",
    )
    scalars.after(small)
    gsent, gkept = call(
        gproj_sum_kernel,
        scalars,
        [(own, whole(part[1:]))] + [(got[j], whole(part[1:])) for j in (1, 2, 3)],
        [((rows, blk), BF, True), ((rows, blk), F32)],
        "gproj_sum",
    )
    gsent = lax.ppermute(gsent, "zh", swap)
    small, _ = barrier((small, gkept))
    sums = [lax.ppermute(small, "x", ring(NX, j)) for j in (1, 2, 3)]
    half_shape = (128, width)
    (grad_hidden,) = call(
        hidden_kernel,
        scalars,
        [
            (summed, whole(half_shape)),
            (inner, whole((1, 128))),
            (student_hidden[0], pl.BlockSpec((128, width), lambda i, s: (0, s[G]))),
            (inverse_rms, whole((128, 1))),
            (norm_gain.reshape(1, D_S), pl.BlockSpec((1, width), lambda i, s: (0, s[G]))),
        ],
        [(half_shape, F32)],
        "hidden",
        pinned=range(1),
    )
    gsent, grad_hidden = barrier((gsent, grad_hidden))
    grad_proj = (gkept + gsent.astype(F32)) / live_count
    *sums, grad_proj = barrier((*sums, grad_proj))
    small = sum(sums, small)
    distill_loss = small[20, 0] / (live_count * D_T)
    gain_rows = lax.dynamic_slice_in_dim(norm_gain.reshape(20, 128), g * 10, 10, 0)
    gain_sums = lax.dynamic_slice_in_dim(small, g * 10, 10, 0)
    grad_gain = (gain_sums / (gain_rows * live_count)).reshape(width)
    return (target[None], distill_loss, grad_proj, grad_gain, grad_hidden[None])


def solution(mesh):
    fine = Mesh(mesh.devices.reshape(2, 4, 4, 2, 2), ("grp", "dp", "x", "zh", "core"))
    in_specs = (
        P("dp", None, MP),
        P("dp", None, None),
        P("dp", None, None),
        P(MP, None),
        P("dp", MP, None),
        P("dp", MP, None),
        P(),
        P(None, ("grp", "dp")),
        P(),
    )
    out_specs = (P("dp", MP, "grp"), P(), P(MP, ("grp", "dp")), P("grp"), P("dp", MP, "grp"))
    return jax.shard_map(body, mesh=fine, in_specs=in_specs, out_specs=out_specs, check_vma=False)
```
